512 devices in a mesh: seq: 32 (over z_lo, x), tp: 8 (over y, core), pool: 2 (over z_hi).
Axes of the slice: x: 4, y: 4, z: 16 (z_hi: 2, z_lo: 8; z = z_hi * 8 + z_lo), core: 2. Of those that a mesh axis runs over, the one named last changes fastest.
Arguments:
- q_pre: bfloat16 [2, 4096, 8192], P('pool', 'seq', 'tp'), may hold values from -102 to 102
- k_pre: bfloat16 [2, 4096, 1024], P('pool', 'seq', 'tp'), may hold values from -10 to 10
- v_pre: bfloat16 [2, 4096, 1024], P('pool', 'seq', 'tp'), may hold values from -6 to 6
- out_weight: bfloat16 [8192, 12288], P('tp', 'seq'), may hold values from -0.0625 to 0.0625
- residual: bfloat16 [2, 4096, 12288], P('pool', 'tp', 'seq'), may hold values from -6 to 6
- span_ids: int32 [2, 32], replicated, may hold values from 0 to 31, each once within a row
- page_counts: int32 [2, 8], replicated, may hold values from 1 to 16, 32 in all within a row
- tail_rows: int32 [2, 8], replicated, may hold values from 1 to 128
- dest_group: int32 [2, 8], replicated, may hold values from 0 to 31, as said below
- dec_q: bfloat16 [2, 8, 4, 8192], P(None, None, None, 'tp'), may hold values from -102 to 102
- dec_k: bfloat16 [2, 8, 4, 1024], P(None, None, None, 'tp'), may hold values from -10 to 10
- dec_v: bfloat16 [2, 8, 4, 1024], P(None, None, None, 'tp'), may hold values from -6 to 6
Outputs:
- mixed: bfloat16 [2, 4096, 12288], P('pool', 'tp', 'seq')
- decoded: bfloat16 [2, 32, 4, 8192], P('pool', 'seq', None, 'tp')
The draws below stay inside these ranges and needn't reach their ends.
Inputs may be any that keep to these rules, and one draw needn't show every extreme that they name: `dest_group`: distinct within a row; 0 and 31 are in every row.
All inputs are finite; a program needn't handle non-finite values.
Results may differ from the reference program's by a relative error of at most 0.01.
Values may be sent and summed in bfloat16 or wider, within the bound.
A program may use at most 64 MiB of HBM per device.

```python
import math
import jax
import jax.numpy as jnp
import numpy as np
from jax import lax

D = 12288
HD = 128
QH = 64
KVH = 8
SPAN = 128
STEPS = 4
TOKENS = 4096
REQS = 8
QF = 8192
KF = 1024
N_SEQ = 32
N_TP = 8
N_POOL = 2


def query_law(key, lead_shape):
    key = jax.random.fold_in(key, 11)
    base = jnp.clip(jax.random.normal(key, lead_shape + (QH, HD), jnp.float32), -6.0, 6.0)
    return base


def key_law(key, lead_shape, salt):
    key = jax.random.fold_in(key, salt)
    base = jnp.clip(jax.random.normal(key, lead_shape + (KVH, HD), jnp.float32), -6.0, 6.0)
    return base


def draw_q_pre(key, part):
    return query_law(key, (N_POOL, TOKENS)).reshape(N_POOL, TOKENS, QH * HD).astype(jnp.bfloat16)


def draw_k_pre(key, part):
    return key_law(key, (N_POOL, TOKENS), 13).reshape(N_POOL, TOKENS, KVH * HD).astype(jnp.bfloat16)


def draw_dec_q(key, part):
    key = jax.random.fold_in(key, 17)
    return query_law(key, (N_POOL, REQS, STEPS)).reshape(N_POOL, REQS, STEPS, QH * HD).astype(jnp.bfloat16)


def draw_dec_k(key, part):
    return key_law(key, (N_POOL, REQS, STEPS), 19).reshape(N_POOL, REQS, STEPS, KVH * HD).astype(jnp.bfloat16)


def draw_dest_group(key, part):
    key = jax.random.fold_in(key, 5)
    picked_rows = []
    for member in range(N_POOL):
        member_key = jax.random.fold_in(key, member)
        inner = jax.random.permutation(jax.random.fold_in(member_key, 1), N_SEQ - 2).astype(jnp.int32) + 1
        picks = jnp.concatenate([jnp.array([0, N_SEQ - 1], jnp.int32), inner[:REQS - 2]])
        shuffle = jax.random.permutation(jax.random.fold_in(member_key, 2), REQS)
        picked_rows.append(picks[shuffle])
    return jnp.stack(picked_rows)


def set_ends(entries, stream_key, least, high):
    index_at = [jax.random.randint(jax.random.fold_in(stream_key, axis), (), 0, length) for axis, length in enumerate(entries.shape)]
    main_axis = entries.shape.index(max(entries.shape))
    neighbour = index_at[:main_axis] + [(index_at[main_axis] + 1) % entries.shape[main_axis]] + index_at[main_axis + 1:]
    return entries.at[tuple(index_at)].set(least).at[tuple(neighbour)].set(high)


def block_levels(own_key, shape, pieces, smallest, top_value):
    loudness = 1.0
    for dim, blocks in pieces:
        draws = jax.random.uniform(jax.random.fold_in(jax.random.fold_in(own_key, 6), dim), (blocks,), jnp.float32, smallest / len(pieces), top_value / len(pieces))
        loudness = loudness * jnp.repeat(jnp.exp(draws), shape[dim] // blocks).reshape((-1,) + (1,) * (len(shape) - 1 - dim))
    return loudness


def split_up(amount, total, most, skew):
    portions = [(1 << 20) // math.isqrt(standing ** skew) + 1 for standing in range(2, amount + 1)]
    surplus, given = total - most - (amount - 1), [1] * (amount - 1)
    while surplus > 0:
        movable = [i for i in range(amount - 1) if given[i] < most]
        whole, left = sum([portions[i] for i in movable]), surplus
        for i in movable:
            extra = min(most - given[i], max(1, left * portions[i] // whole), surplus)
            given[i] = given[i] + extra
            surplus = surplus - extra
    return np.array([most] + given)


def ragged_sizes(key, amount, total, limit, skew):
    if amount == 2:
        one = jax.random.randint(key, (), max(1, total - limit), min(limit, total - 1) + 1)
        return jnp.stack([one, total - one])
    lengths = jnp.asarray(split_up(amount, total, limit, skew), jnp.int32)
    twos = (amount - 1) // 2
    giver, sink = lengths[1:1 + 2 * twos:2], lengths[2:2 + 2 * twos:2]
    room = jnp.minimum(giver - 1, limit - sink)
    moved = jax.random.randint(jax.random.fold_in(key, 1), (twos,), 0, 1 << 20) % (room + 1)
    lengths = lengths.at[1:1 + 2 * twos:2].set(giver - moved).at[2:2 + 2 * twos:2].set(sink + moved)
    return lengths[jax.random.permutation(jax.random.fold_in(key, 2), amount)]


def gaussian(own_key, extent, scale, reach, cuts=(), kind=jnp.bfloat16):
    factor_of = block_levels(own_key, extent, cuts, -0.22, 0.18) if cuts else 1.0
    values = jax.random.normal(own_key, extent, jnp.float32) * scale * factor_of
    return jnp.minimum(jnp.maximum(values, -reach), reach).astype(kind)


def setup_inputs(seed: int = 0) -> dict:
    key_of = jax.random.split(jax.random.key(seed), 13)
    q_pre = draw_q_pre(jax.random.fold_in(key_of[12], 71), 0)
    k_pre = draw_k_pre(jax.random.fold_in(key_of[12], 71), 0)
    v_pre = gaussian(key_of[2], (N_POOL, TOKENS, KF), 1.0, 6.0, ((0, 2), (1, 32), (2, 8)))
    out_weight = gaussian(key_of[3], (QF, D), QF ** -0.5, 0.0625, ((0, 8), (1, 32)))
    residual = gaussian(key_of[4], (N_POOL, TOKENS, D), 1.0, 6.0, ((0, 2), (1, 8), (2, 32)))
    span_ids = jax.vmap(lambda own: jax.random.permutation(own, N_SEQ))(jax.random.split(key_of[5], N_POOL)).reshape((N_POOL, N_SEQ)).astype(jnp.int32)
    page_counts = jax.vmap(lambda own: ragged_sizes(own, REQS, N_SEQ, N_SEQ // 2, 2))(jax.random.split(key_of[6], N_POOL)).reshape((N_POOL, REQS)).astype(jnp.int32)
    tail_rows = set_ends(jax.random.randint(key_of[7], (N_POOL, REQS), 1, SPAN + 1), jax.random.fold_in(key_of[7], 1), 1, SPAN).astype(jnp.int32)
    dest_group = draw_dest_group(jax.random.fold_in(key_of[12], 71), 0)
    dec_q = draw_dec_q(jax.random.fold_in(key_of[12], 71), 0)
    dec_k = draw_dec_k(jax.random.fold_in(key_of[12], 71), 0)
    dec_v = gaussian(key_of[11], (N_POOL, REQS, STEPS, KF), 1.0, 6.0, ((3, 8),))
    return {"q_pre": q_pre, "k_pre": k_pre, "v_pre": v_pre, "out_weight": out_weight, "residual": residual, "span_ids": span_ids, "page_counts": page_counts, "tail_rows": tail_rows, "dest_group": dest_group, "dec_q": dec_q, "dec_k": dec_k, "dec_v": dec_v}


NEG_FILL = -1e+30

def span_request(counts, page_pos):
    ends_incl = jnp.cumsum(counts)
    return lax.optimization_barrier(jnp.sum((ends_incl[None, :] <= page_pos[:, None]).astype(jnp.int32), axis=1))

def token_layout(span_row, counts):
    token_ids = jnp.arange(TOKENS, dtype=jnp.int32)
    page_of = span_row[token_ids // SPAN]
    position = page_of * SPAN + token_ids % SPAN
    request = span_request(counts, page_of)
    return (position, request)

def prefill_attention(queries, keys, values, position, request):
    repeat = QH // KVH
    score_scale = 1.0 / math.sqrt(HD)
    block_len = math.gcd(512, TOKENS)
    grouped_q = queries.reshape(TOKENS, KVH, repeat, HD)
    grouped_k = keys.reshape(TOKENS, KVH, HD)
    grouped_v = values.reshape(TOKENS, KVH, HD)

    def per_head(kv_head):
        head_k = lax.dynamic_index_in_dim(grouped_k, kv_head, 1, keepdims=False).astype(jnp.float32)
        head_v = lax.dynamic_index_in_dim(grouped_v, kv_head, 1, keepdims=False).astype(jnp.float32)
        head_q = lax.dynamic_index_in_dim(grouped_q, kv_head, 1, keepdims=False)

        def per_block(block_no):
            first_row = block_no * block_len
            block_q = lax.dynamic_slice_in_dim(head_q, first_row, block_len, 0).astype(jnp.float32)
            block_pos = lax.dynamic_slice_in_dim(position, first_row, block_len, 0)
            block_req = lax.dynamic_slice_in_dim(request, first_row, block_len, 0)
            visible = (block_req[:, None] == request[None, :]) & (position[None, :] <= block_pos[:, None])
            visible = visible[:, None, :]
            scores = jnp.einsum('qrd,kd->qrk', block_q, head_k) * score_scale
            scores = jnp.where(visible, scores, NEG_FILL)
            highest = lax.optimization_barrier(jnp.max(scores, axis=2, keepdims=True))
            weights = jnp.where(visible, jnp.exp(scores - highest), 0.0)
            denominator = lax.optimization_barrier(jnp.sum(weights, axis=2, keepdims=True))
            rounded = lax.optimization_barrier(weights.astype(jnp.bfloat16)).astype(jnp.float32)
            return (jnp.einsum('qrk,kd->qrd', rounded, head_v) / denominator).astype(jnp.bfloat16)
        blocks = lax.map(per_block, jnp.arange(TOKENS // block_len, dtype=jnp.int32))
        return blocks.reshape(TOKENS, repeat, HD)
    heads_out = lax.map(per_head, jnp.arange(KVH, dtype=jnp.int32))
    return jnp.transpose(heads_out, (1, 0, 2, 3)).reshape(TOKENS, QH * HD)

def project_rows(attention, out_weight, residual):
    width = QH * HD // N_TP
    summed = jnp.zeros((TOKENS, D), jnp.float32)
    for source in range(N_TP):
        partial_sum = jnp.dot(attention[:, source * width:(source + 1) * width], out_weight[source * width:(source + 1) * width], preferred_element_type=jnp.float32)
        summed = summed + lax.optimization_barrier(partial_sum.astype(jnp.bfloat16)).astype(jnp.float32)
    return (summed + residual.astype(jnp.float32)).astype(jnp.bfloat16)

def decode_prompt(keys, values, position, request, counts, tails, dec_queries, dec_keys, dec_values):
    repeat = QH // KVH
    score_scale = 1.0 / math.sqrt(HD)
    ends_incl = jnp.cumsum(counts)
    starts = (ends_incl - counts) * SPAN
    live_rows = (counts - 1) * SPAN + tails
    prompt_k = keys.reshape(TOKENS, KVH, HD).astype(jnp.float32)
    prompt_v = values.reshape(TOKENS, KVH, HD).astype(jnp.float32)
    steps_at = jnp.arange(STEPS, dtype=jnp.int32)
    causal = (steps_at[None, :] <= steps_at[:, None])[:, None, None, :]

    def per_request(req_no):
        visible = (request == req_no) & (position - starts[req_no] < live_rows[req_no])
        visible = visible[None, None, None, :]
        query_rows = dec_queries[req_no].reshape(STEPS, KVH, repeat, HD).astype(jnp.float32)
        new_keys = dec_keys[req_no].reshape(STEPS, KVH, HD).astype(jnp.float32)
        new_values = dec_values[req_no].reshape(STEPS, KVH, HD).astype(jnp.float32)
        old_scores = jnp.einsum('sgrd,tgd->sgrt', query_rows, prompt_k) * score_scale
        old_scores = jnp.where(visible, old_scores, NEG_FILL)
        new_scores = jnp.einsum('sgrd,jgd->sgrj', query_rows, new_keys) * score_scale
        new_scores = jnp.where(causal, new_scores, NEG_FILL)
        highest = jnp.maximum(lax.optimization_barrier(jnp.max(old_scores, axis=3)), lax.optimization_barrier(jnp.max(new_scores, axis=3)))[..., None]
        old_weights = jnp.where(visible, jnp.exp(old_scores - highest), 0.0)
        new_weights = jnp.where(causal, jnp.exp(new_scores - highest), 0.0)
        denominator = lax.optimization_barrier(jnp.sum(old_weights, axis=3, keepdims=True)) + lax.optimization_barrier(jnp.sum(new_weights, axis=3, keepdims=True))
        old_round = lax.optimization_barrier(old_weights.astype(jnp.bfloat16)).astype(jnp.float32)
        new_round = lax.optimization_barrier(new_weights.astype(jnp.bfloat16)).astype(jnp.float32)
        result = (jnp.einsum('sgrt,tgd->sgrd', old_round, prompt_v) + jnp.einsum('sgrj,jgd->sgrd', new_round, new_values)) / denominator
        return result.reshape(STEPS, QH * HD).astype(jnp.bfloat16)
    return lax.map(per_request, jnp.arange(REQS, dtype=jnp.int32))

def reference(q_pre, k_pre, v_pre, out_weight, residual, span_ids, page_counts, tail_rows, dest_group, dec_q, dec_k, dec_v):
    mixed_rows = []
    decoded_rows = [None, None]
    for prompt in range(N_POOL):
        position, request = token_layout(span_ids[prompt], page_counts[prompt])
        attention = prefill_attention(q_pre[prompt], k_pre[prompt], v_pre[prompt], position, request)
        mixed_rows.append(project_rows(attention, out_weight, residual[prompt]))
        results = decode_prompt(k_pre[prompt], v_pre[prompt], position, request, page_counts[prompt], tail_rows[prompt], dec_q[prompt], dec_k[prompt], dec_v[prompt])
        holder = jnp.zeros((N_SEQ, STEPS, QH * HD), jnp.bfloat16).at[dest_group[prompt]].set(results)
        decoded_rows[N_POOL - 1 - prompt] = holder
    return (jnp.stack(mixed_rows), jnp.stack(decoded_rows))
```

```python
import functools
import math

import jax
import jax.numpy as jnp
from jax import lax
from jax.experimental import pallas as pl
from jax.experimental.pallas import tpu as pltpu
from jax.sharding import PartitionSpec as P

HD = 128
QH = 64
KVH = 8
X_SIZE = 4
NEG_FILL = -1e30
LOG2E = 1.4426950408889634
MESH = pl.DeviceIdType.MESH
F32 = jnp.float32
BF16 = jnp.bfloat16


def remote(src, dst, send_sem, recv_sem, seq):
    return pltpu.make_async_remote_copy(
        src_ref=src,
        dst_ref=dst,
        send_sem=send_sem,
        recv_sem=recv_sem,
        device_id={"seq": seq},
        device_id_type=MESH,
    )


def gather_kernel(
    nz, first_ref, second_ref, out_ref, z_send, z_recv, x_send, x_recv, far_send, far_recv
):
    me = lax.axis_index("seq")
    z, x = me // X_SIZE, me % X_SIZE
    right = z * X_SIZE + (x + 1) % X_SIZE
    left = z * X_SIZE + (x + 3) % X_SIZE
    opposite = (x + 2) % X_SIZE

    barrier = pltpu.get_barrier_semaphore()
    for seq in (right, left):
        pl.semaphore_signal(barrier, inc=1, device_id={"seq": seq}, device_id_type=MESH)

    @pl.when(z > 0)
    def _():
        pl.semaphore_signal(barrier, inc=1, device_id={"seq": me - X_SIZE}, device_id_type=MESH)

    @pl.when(z < nz - 1)
    def _():
        pl.semaphore_signal(barrier, inc=1, device_id={"seq": me + X_SIZE}, device_id_type=MESH)

    out_ref[me, 0] = first_ref[...]
    out_ref[me, 1] = second_ref[...]
    peers = 2 + jnp.where(z > 0, 1, 0) + jnp.where(z < nz - 1, 1, 0)
    pl.semaphore_wait(barrier, peers)

    def z_copy(block_z, direction, target):
        slot = out_ref.at[block_z * X_SIZE + x]
        return remote(slot, slot, z_send.at[direction, block_z], z_recv.at[block_z], target)

    def x_copy(block_z, block_x, direction, target):
        slot = out_ref.at[block_z * X_SIZE + block_x]
        return remote(
            slot, slot, x_send.at[direction, block_z], x_recv.at[direction, block_z], target
        )

    def far_copy(block_z, block_x, direction, target):
        slot = out_ref.at[block_z * X_SIZE + block_x, direction]
        return remote(
            slot, slot, far_send.at[direction, block_z], far_recv.at[direction, block_z], target
        )

    def spread(block_z):
        x_copy(block_z, x, 0, right).start()
        x_copy(block_z, x, 1, left).start()

    def relay(block_z):
        x_copy(block_z, (x + 3) % X_SIZE, 0, right).wait_recv()
        far_copy(block_z, (x + 3) % X_SIZE, 0, right).start()
        x_copy(block_z, (x + 1) % X_SIZE, 1, left).wait_recv()
        far_copy(block_z, (x + 1) % X_SIZE, 1, left).start()

    def step(t, carry):
        low, high = z - t, z + t

        @pl.when((t > 0) & (low >= 0))
        def _():
            z_copy(low, 0, me).wait_recv()

        @pl.when((low >= 0) & (z < nz - 1))
        def _():
            z_copy(low, 0, me + X_SIZE).start()

        @pl.when((t > 0) & (high < nz))
        def _():
            z_copy(high, 1, me).wait_recv()

        @pl.when((high < nz) & (z > 0))
        def _():
            z_copy(high, 1, me - X_SIZE).start()

        @pl.when(low >= 0)
        def _():
            spread(low)

        @pl.when((t > 0) & (high < nz))
        def _():
            spread(high)

        @pl.when((t > 0) & (low + 1 >= 0))
        def _():
            relay(low + 1)

        @pl.when((t > 1) & (high - 1 < nz))
        def _():
            relay(high - 1)

        return carry

    lax.fori_loop(0, nz + 1, step, 0)

    def drain(block_z, carry):
        @pl.when((block_z <= z) & (z < nz - 1))
        def _():
            z_copy(block_z, 0, me).wait_send()

        @pl.when((block_z >= z) & (z > 0))
        def _():
            z_copy(block_z, 1, me).wait_send()

        x_copy(block_z, x, 0, right).wait_send()
        x_copy(block_z, x, 1, left).wait_send()
        far_copy(block_z, opposite, 0, right).wait()
        far_copy(block_z, opposite, 1, left).wait()
        return carry

    lax.fori_loop(0, nz, drain, 0)


def gather_seq(first, second, count, collective_id):
    nz = count // X_SIZE
    rows, columns = first.shape
    dma = pltpu.SemaphoreType.DMA
    return pl.pallas_call(
        functools.partial(gather_kernel, nz),
        out_shape=jax.ShapeDtypeStruct((count, 2, rows, columns), first.dtype),
        in_specs=[pl.BlockSpec(memory_space=pltpu.VMEM)] * 2,
        out_specs=pl.BlockSpec(memory_space=pltpu.VMEM),
        scratch_shapes=[dma((2, nz)), dma((nz,)), dma((2, nz)), dma((2, nz)), dma((2, nz)), dma((2, nz))],
        compiler_params=pltpu.CompilerParams(
            collective_id=collective_id, has_side_effects=True, vmem_limit_bytes=40 << 20
        ),
    )(first, second)


def matmul_nt(a, b):
    return lax.dot_general(a, b, (((1,), (1,)), ((), ())), preferred_element_type=F32)


def matmul_tn(a, b):
    return lax.dot_general(a, b, (((0,), (0,)), ((), ())), preferred_element_type=F32)


CHUNK = 4


def attend_kernel(
    span_ref,
    counts_ref,
    tails_ref,
    dest_ref,
    q_ref,
    kv_ref,
    dq_ref,
    dk_ref,
    dv_ref,
    out_ref,
    dec_ref,
    place,
    dec_rows,
    new_page,
):
    pool_at = lax.axis_index("pool")
    seq_at = lax.axis_index("seq")
    pages, span = kv_ref.shape[0], kv_ref.shape[2]
    requests = counts_ref.shape[1]
    steps = dec_ref.shape[0]
    repeat = QH // KVH
    factor = LOG2E / math.sqrt(HD)
    keys = CHUNK * span

    def invert(j, carry):
        place[span_ref[pool_at, j]] = j
        return carry

    lax.fori_loop(0, pages, invert, 0)

    own = span_ref[pool_at, seq_at]
    begin = jnp.int32(0)
    first = jnp.int32(0)
    dec_first, dec_count, dec_tail, dec_no, holds = (jnp.int32(0),) * 5
    for r in range(requests):
        count = counts_ref[pool_at, r]
        first = jnp.where(begin <= own, begin, first)
        match = dest_ref[pool_at, r] == seq_at
        dec_first = jnp.where(match, begin, dec_first)
        dec_count = jnp.where(match, count, dec_count)
        dec_tail = jnp.where(match, tails_ref[pool_at, r], dec_tail)
        dec_no = jnp.where(match, r, dec_no)
        holds = jnp.where(match, 1, holds)
        begin = begin + count

    def load(which, page, last):
        return jnp.concatenate(
            [kv_ref[place[jnp.minimum(page + j, last)], which] for j in range(CHUNK)], axis=0
        )

    last_chunk = (own - first) // CHUNK
    width = 2 * HD
    ahead = lax.broadcasted_iota(jnp.int32, (keys, width), 0) - (
        lax.broadcasted_iota(jnp.int32, (keys, width), 1) % span
    )
    visible = ahead <= (own - first - last_chunk * CHUNK) * span
    for pair in range(repeat // 2):
        heads = [2 * pair, 2 * pair + 1]
        rows = jnp.concatenate([q_ref[:, h * HD : (h + 1) * HD] for h in heads], axis=0)

        page = first + last_chunk * CHUNK
        scores = jnp.where(visible, matmul_nt(load(0, page, own), rows), NEG_FILL)
        highest = jnp.max(scores, axis=0, keepdims=True)
        weights = jnp.exp2((scores - highest) * factor)
        total = jnp.sum(weights, axis=0, keepdims=True)
        accum = matmul_tn(load(1, page, own), weights.astype(BF16))

        def chunk(i, state):
            highest, total, accum = state
            page = first + i * CHUNK
            scores = matmul_nt(load(0, page, own), rows)
            new_high = jnp.maximum(highest, jnp.max(scores, axis=0, keepdims=True))
            weights = jnp.exp2((scores - new_high) * factor)
            fade = jnp.exp2((highest - new_high) * factor)
            total = total * fade + jnp.sum(weights, axis=0, keepdims=True)
            accum = accum * fade + matmul_tn(load(1, page, own), weights.astype(BF16))
            return (new_high, total, accum)

        highest, total, accum = lax.fori_loop(0, last_chunk, chunk, (highest, total, accum))
        result = accum / total
        for n, h in enumerate(heads):
            out_ref[:, h * HD : (h + 1) * HD] = jnp.transpose(
                result[:, n * HD : (n + 1) * HD]
            ).astype(BF16)

    @pl.when(holds == 0)
    def _():
        dec_ref[...] = jnp.zeros_like(dec_ref)

    @pl.when(holds == 1)
    def _():
        queries = dq_ref[pool_at, dec_no].astype(F32)
        for h in range(repeat):
            dec_rows[h * steps : (h + 1) * steps, :] = queries[:, h * HD : (h + 1) * HD]
        rows = dec_rows[...].astype(BF16)
        new_page[...] = jnp.zeros_like(new_page)
        new_page[0, :steps, :] = dk_ref[pool_at, dec_no].astype(F32)
        new_page[1, :steps, :] = dv_ref[pool_at, dec_no].astype(F32)

        count = rows.shape[0]
        step_of = lax.broadcasted_iota(jnp.int32, (count, span), 0) % steps
        causal = lax.broadcasted_iota(jnp.int32, (count, span), 1) <= step_of
        scores = jnp.where(causal, matmul_nt(rows, new_page[0].astype(BF16)), NEG_FILL)
        highest = jnp.max(scores, axis=1, keepdims=True)
        weights = jnp.exp2((scores - highest) * factor)
        total = jnp.sum(weights, axis=1, keepdims=True)
        accum = jnp.dot(
            weights.astype(BF16), new_page[1].astype(BF16), preferred_element_type=F32
        )
        live = (dec_count - 1) * span + dec_tail
        last = dec_first + dec_count - 1
        key_no = lax.broadcasted_iota(jnp.int32, (count, keys), 1)

        def chunk(i, state):
            highest, total, accum = state
            page = dec_first + i * CHUNK
            scores = matmul_nt(rows, load(0, page, last))
            scores = jnp.where(key_no < live - i * keys, scores, NEG_FILL)
            new_high = jnp.maximum(highest, jnp.max(scores, axis=1, keepdims=True))
            weights = jnp.exp2((scores - new_high) * factor)
            fade = jnp.exp2((highest - new_high) * factor)
            total = total * fade + jnp.sum(weights, axis=1, keepdims=True)
            accum = accum * fade + jnp.dot(
                weights.astype(BF16), load(1, page, last), preferred_element_type=F32
            )
            return (new_high, total, accum)

        state = lax.fori_loop(0, (dec_count + CHUNK - 1) // CHUNK, chunk, (highest, total, accum))
        dec_rows[...] = state[2] / state[1]
        for h in range(repeat):
            dec_ref[:, h * HD : (h + 1) * HD] = dec_rows[h * steps : (h + 1) * steps, :].astype(
                BF16
            )


def attend(span_ids, page_counts, tail_rows, dest_group, q, kv, dec_q, dec_k, dec_v):
    steps = dec_q.shape[2]
    span = q.shape[0]
    smem = pl.BlockSpec(memory_space=pltpu.SMEM)
    vmem = pl.BlockSpec(memory_space=pltpu.VMEM)
    return pl.pallas_call(
        attend_kernel,
        out_shape=(
            jax.ShapeDtypeStruct(q.shape, BF16),
            jax.ShapeDtypeStruct((steps, q.shape[1]), BF16),
        ),
        in_specs=[smem] * 4 + [vmem] * 5,
        out_specs=(vmem, vmem),
        scratch_shapes=[
            pltpu.SMEM((kv.shape[0],), jnp.int32),
            pltpu.VMEM((steps * (QH // KVH), HD), F32),
            pltpu.VMEM((2, span, HD), F32),
        ],
        compiler_params=pltpu.CompilerParams(vmem_limit_bytes=40 << 20),
    )(span_ids, page_counts, tail_rows, dest_group, q, kv, dec_q, dec_k, dec_v)


def per_device(
    q_pre,
    k_pre,
    v_pre,
    out_weight,
    residual,
    span_ids,
    page_counts,
    tail_rows,
    dest_group,
    dec_q,
    dec_k,
    dec_v,
):
    seq_count = lax.axis_size("seq")
    tp_count = lax.axis_size("tp")
    kv = gather_seq(k_pre[0], v_pre[0], seq_count, 0)
    attention, answers = attend(
        span_ids, page_counts, tail_rows, dest_group, q_pre[0], kv, dec_q, dec_k, dec_v
    )
    decoded = lax.ppermute(answers, "pool", [(0, 1), (1, 0)])[None, None]

    half = attention.shape[0] // 2
    rows = gather_seq(attention[:half], attention[half:], seq_count, 1)
    partial_rows = jnp.dot(
        rows.reshape(-1, rows.shape[3]), out_weight, preferred_element_type=F32
    ).astype(BF16)
    tok_rows = residual.shape[1]
    arrived = lax.all_to_all(
        partial_rows.reshape(tp_count, tok_rows, -1), "tp", split_axis=0, concat_axis=0, tiled=True
    )
    summed = arrived[0].astype(F32)
    for source in range(1, tp_count):
        summed = summed + arrived[source].astype(F32)
    mixed = (summed + residual[0].astype(F32)).astype(BF16)[None]
    return (mixed, decoded)


def solution(mesh):
    placed = (
        P("pool", "seq", "tp"),
        P("pool", "seq", "tp"),
        P("pool", "seq", "tp"),
        P("tp", "seq"),
        P("pool", "tp", "seq"),
        P(),
        P(),
        P(),
        P(),
        P(None, None, None, "tp"),
        P(None, None, None, "tp"),
        P(None, None, None, "tp"),
    )
    return jax.shard_map(
        per_device,
        mesh=mesh,
        in_specs=placed,
        out_specs=(P("pool", "tp", "seq"), P("pool", "seq", None, "tp")),
        check_vma=False,
    )
```

```python
import math

import jax
import jax.numpy as jnp
from jax import lax
from jax.experimental import pallas as pl
from jax.experimental.pallas import tpu as pltpu
from jax.sharding import PartitionSpec as P

HD = 128
QH = 64
KVH = 8
REPEAT = QH // KVH
NX = 4
NEG_FILL = -1e30
FAR_FILL = 1e30
FACTOR = math.log2(math.e) / math.sqrt(HD)
MESH = pl.DeviceIdType.MESH
F32 = jnp.float32
BF16 = jnp.bfloat16
W_PIECES = 4


def matmul_nt(a, b):
    return lax.dot_general(a, b, (((1,), (1,)), ((), ())), preferred_element_type=F32)


def matmul_tn(a, b):
    return lax.dot_general(a, b, (((0,), (0,)), ((), ())), preferred_element_type=F32)


def remote(src, dst, send_sem, recv_sem, **target):
    return pltpu.make_async_remote_copy(
        src_ref=src,
        dst_ref=dst,
        send_sem=send_sem,
        recv_sem=recv_sem,
        device_id=target,
        device_id_type=MESH,
    )


def kernel(
    span_ref,
    counts_ref,
    tails_ref,
    dest_ref,
    dq_ref,
    dk_ref,
    dv_ref,
    k_hbm,
    v_hbm,
    q_hbm,
    w_hbm,
    res_hbm,
    out_ref,
    dec_ref,
    kv,
    q_in,
    rows_of,
    high_of,
    total_of,
    accum,
    heads_out,
    weight,
    resid,
    core_out,
    core_in,
    stash,
    y_out,
    relay_in,
    owner_in,
    x_out,
    x_in,
    dec_rows,
    new_page,
    dec_out,
    dec_in,
    local_sem,
    kz_send,
    kz_recv,
    kx_send,
    kx_recv,
    kf_send,
    kf_recv,
    wx_send,
    wx_recv,
    wf_send,
    wf_recv,
    az_send,
    az_recv,
    core_send,
    core_recv,
    y_send,
    relay_recv,
    owner_recv,
    x_send,
    x_recv,
    pool_send,
    pool_recv,
):
    me = lax.axis_index("seq")
    tp_at = lax.axis_index("tp")
    pool_at = lax.axis_index("pool")
    nz = kv.shape[0] // NX
    ny = NX
    span = kv.shape[2]
    z, x = me // NX, me % NX
    y, core = tp_at // 2, tp_at % 2
    right, left = z * NX + (x + 1) % NX, z * NX + (x + 3) % NX
    opposite = (x + 2) % NX
    sibling = tp_at + 1 - 2 * core
    part = heads_out.shape[2]
    steps = dec_ref.shape[0]
    requests = counts_ref.shape[1]

    load_k = pltpu.make_async_copy(k_hbm, kv.at[me, 0], local_sem.at[0])
    load_v = pltpu.make_async_copy(v_hbm, kv.at[me, 1], local_sem.at[1])
    load_q = pltpu.make_async_copy(q_hbm, q_in, local_sem.at[2])
    load_w = pltpu.make_async_copy(w_hbm, weight.at[x], local_sem.at[3])
    load_r = pltpu.make_async_copy(res_hbm, resid, local_sem.at[4])
    for load in (load_k, load_v, load_q, load_w, load_r):
        load.start()

    barrier = pltpu.get_barrier_semaphore()

    def greet(**target):
        pl.semaphore_signal(barrier, inc=1, device_id=target, device_id_type=MESH)

    for distance in range(1, NX):
        greet(seq=z * NX + (x + distance) % NX)
        greet(tp=((y + distance) % ny) * 2 + core)
    greet(tp=sibling)
    greet(pool=1 - pool_at)

    @pl.when(z > 0)
    def _():
        greet(seq=me - NX)

    @pl.when(z < nz - 1)
    def _():
        greet(seq=me + NX)

    load_k.wait()
    load_v.wait()
    pl.semaphore_wait(barrier, 8 + jnp.where(z > 0, 1, 0) + jnp.where(z < nz - 1, 1, 0))

    def kz_copy(zb, direction, target):
        slot = kv.at[zb * NX + x]
        return remote(slot, slot, kz_send.at[direction, zb], kz_recv.at[zb], seq=target)

    def kx_copy(zb, xb, direction, target):
        slot = kv.at[zb * NX + xb]
        return remote(
            slot, slot, kx_send.at[direction, zb], kx_recv.at[direction, zb], seq=target
        )

    def kf_copy(zb, xb, direction, target):
        slot = kv.at[zb * NX + xb, direction]
        return remote(
            slot, slot, kf_send.at[direction, zb], kf_recv.at[direction, zb], seq=target
        )

    def spread(zb):
        kx_copy(zb, x, 0, right).start()
        kx_copy(zb, x, 1, left).start()

    def relay(zb):
        kx_copy(zb, (x + 3) % NX, 0, right).wait_recv()
        kf_copy(zb, (x + 3) % NX, 0, right).start()
        kx_copy(zb, (x + 1) % NX, 1, left).wait_recv()
        kf_copy(zb, (x + 1) % NX, 1, left).start()

    height = weight.shape[1] // W_PIECES

    def w_piece(xb, piece):
        return weight.at[xb, pl.ds(piece * height, height)]

    def wx_copy(xb, piece, direction, target):
        slot = w_piece(xb, piece)
        return remote(
            slot, slot, wx_send.at[direction, piece], wx_recv.at[direction, piece], seq=target
        )

    def wf_copy(xb, n, direction, target):
        slot = w_piece(xb, direction * (W_PIECES // 2) + n)
        return remote(
            slot, slot, wf_send.at[direction, n], wf_recv.at[direction, n], seq=target
        )

    def spread_weight():
        load_w.wait()
        for n in range(W_PIECES):
            wx_copy(x, n, 0, right).start()
            wx_copy(x, (n + W_PIECES // 2) % W_PIECES, 1, left).start()

    def relay_weight(n):
        wx_copy((x + 3) % NX, n, 0, right).wait_recv()
        wf_copy((x + 3) % NX, n, 0, right).start()
        wx_copy((x + 1) % NX, n + W_PIECES // 2, 1, left).wait_recv()
        wf_copy((x + 1) % NX, n, 1, left).start()

    def finish_weight():
        for n in range(W_PIECES):
            if n >= W_PIECES // 2:
                wx_copy((x + 3) % NX, n, 0, right).wait_recv()
            else:
                wx_copy((x + 1) % NX, n, 1, left).wait_recv()
        for n in range(W_PIECES // 2):
            wf_copy(opposite, n, 0, right).wait_recv()
            wf_copy(opposite, n, 1, left).wait_recv()

    own = span_ref[pool_at, me]
    begin = jnp.int32(0)
    first = jnp.int32(0)
    dec_first, dec_count, dec_tail, dec_no, holds = (jnp.int32(0),) * 5
    for r in range(requests):
        count = counts_ref[pool_at, r]
        first = jnp.where(begin <= own, begin, first)
        match = dest_ref[pool_at, r] == me
        dec_first = jnp.where(match, begin, dec_first)
        dec_count = jnp.where(match, count, dec_count)
        dec_tail = jnp.where(match, tails_ref[pool_at, r], dec_tail)
        dec_no = jnp.where(match, r, dec_no)
        holds = jnp.where(match, 1, holds)
        begin = begin + count

    width = 2 * HD

    def attend(zb, diagonal):
        keys = kv[pl.ds(zb * NX, NX), 0].reshape(NX * span, HD)
        values = kv[pl.ds(zb * NX, NX), 1].reshape(NX * span, HD)
        pages = [span_ref[pool_at, zb * NX + j] for j in range(NX)]
        if diagonal:
            ahead = lax.broadcasted_iota(jnp.int32, (span, width), 0) - (
                lax.broadcasted_iota(jnp.int32, (span, width), 1) % span
            )
        for pair in range(REPEAT // 2):
            scores = matmul_nt(keys, rows_of[pair])
            blocks = [scores[j * span : (j + 1) * span] for j in range(NX)]
            if diagonal:
                blocks = [
                    jnp.where(
                        ahead <= jnp.where(page >= first, (own - page) * span, -2 * span),
                        block,
                        NEG_FILL,
                    )
                    for page, block in zip(pages, blocks)
                ]
                peaks = [jnp.max(block, axis=0, keepdims=True) for block in blocks]
            else:
                seen = [(page >= first) & (page < own) for page in pages]
                peaks = [
                    jnp.where(is_seen, jnp.max(block, axis=0, keepdims=True), NEG_FILL)
                    for is_seen, block in zip(seen, blocks)
                ]
            new_high = jnp.maximum(
                jnp.maximum(peaks[0], peaks[1]), jnp.maximum(peaks[2], peaks[3])
            )
            if not diagonal:
                old_high = high_of[pair, 0:1]
                new_high = jnp.maximum(new_high, old_high)
            weights = []
            sums = []
            for j, block in enumerate(blocks):
                base = new_high if diagonal else jnp.where(seen[j], new_high, FAR_FILL)
                weights.append(jnp.exp2((block - base) * FACTOR))
                sums.append(jnp.sum(weights[-1], axis=0, keepdims=True))
            total = (sums[0] + sums[1]) + (sums[2] + sums[3])
            update = matmul_tn(values, jnp.concatenate(weights, axis=0).astype(BF16))
            if not diagonal:
                fade = jnp.exp2((old_high - new_high) * FACTOR)
                total = total + total_of[pair, 0:1] * fade
                update = update + accum[pair] * fade
            high_of[pair, 0:1] = new_high
            total_of[pair, 0:1] = total
            accum[pair] = update

    lag = 1 + jnp.where((z > 0) & (z < nz - 1), 1, 0) + jnp.where((z > 1) & (z < nz - 2), 1, 0)

    load_q.wait()
    for pair in range(REPEAT // 2):
        for n in range(2):
            h = 2 * pair + n
            rows_of[pair, n * span : (n + 1) * span, :] = q_in[:, h * HD : (h + 1) * HD]

    def far_wait(zb):
        kf_copy(zb, opposite, 0, right).wait_recv()
        kf_copy(zb, opposite, 1, left).wait_recv()

    def gather_step(t, carry):
        low, high = z - t, z + t

        @pl.when((t > 0) & (low >= 0))
        def _():
            kz_copy(low, 0, me).wait_recv()

        @pl.when((low >= 0) & (z < nz - 1))
        def _():
            kz_copy(low, 0, me + NX).start()

        @pl.when((t > 0) & (high < nz))
        def _():
            kz_copy(high, 1, me).wait_recv()

        @pl.when((high < nz) & (z > 0))
        def _():
            kz_copy(high, 1, me - NX).start()

        @pl.when(low >= 0)
        def _():
            spread(low)

        @pl.when((t > 0) & (high < nz))
        def _():
            spread(high)

        past = t - lag

        @pl.when((past >= 0) & (z - past >= 0))
        def _():
            relay(z - past)

        @pl.when((past > 0) & (z + past < nz))
        def _():
            relay(z + past)

        @pl.when(t == nz)
        def _():
            spread_weight()

        ready = t - lag - 2

        @pl.when(ready == 0)
        def _():
            far_wait(z)
            attend(z, True)

        for sign in (-1, 1):
            zb = z + sign * ready

            @pl.when((ready > 0) & (zb >= 0) & (zb < nz))
            def _():
                far_wait(zb)
                attend(zb, False)

        return carry

    lax.fori_loop(0, nz + 3, gather_step, 0)

    for pair in range(REPEAT // 2):
        result = accum[pair] / total_of[pair, 0:1]
        for n in range(2):
            h = 2 * pair + n
            block = jnp.transpose(result[:, n * span : (n + 1) * span]).astype(BF16)
            for s in range(2):
                heads_out[z, s, :, h * HD : (h + 1) * HD] = block[s * part : (s + 1) * part]

    def az_copy(zb, s, direction, target):
        slot = heads_out.at[zb, s]
        return remote(slot, slot, az_send.at[direction, zb, s], az_recv.at[zb, s], seq=target)

    def z_step(t, carry):
        low, high = z - t, z + t
        for s in range(2):

            @pl.when((t > 0) & (low >= 0))
            def _():
                az_copy(low, s, 0, me).wait_recv()

            @pl.when((low >= 0) & (z < nz - 1))
            def _():
                az_copy(low, s, 0, me + NX).start()

            @pl.when((t > 0) & (high < nz))
            def _():
                az_copy(high, s, 1, me).wait_recv()

            @pl.when((high < nz) & (z > 0))
            def _():
                az_copy(high, s, 1, me - NX).start()

        return carry

    z_step(0, 0)

    queries = dq_ref[pool_at, dec_no].astype(F32)
    for h in range(REPEAT):
        dec_rows[h * steps : (h + 1) * steps, :] = queries[:, h * HD : (h + 1) * HD]
    rows = dec_rows[...].astype(BF16)
    new_page[...] = jnp.zeros_like(new_page)
    new_page[0, :steps, :] = dk_ref[pool_at, dec_no].astype(F32)
    new_page[1, :steps, :] = dv_ref[pool_at, dec_no].astype(F32)
    row_count = rows.shape[0]
    lane = lax.broadcasted_iota(jnp.int32, (row_count, span), 1)
    step_of = lax.broadcasted_iota(jnp.int32, (row_count, span), 0) % steps
    new_scores = jnp.where(
        lane <= step_of, matmul_nt(rows, new_page[0].astype(BF16)), NEG_FILL
    )
    live = (dec_count - 1) * span + dec_tail
    old_scores = []
    for zb in range(nz):
        keys = kv[zb * NX : (zb + 1) * NX, 0].reshape(NX * span, HD)
        scores = matmul_nt(rows, keys)
        for j in range(NX):
            page = span_ref[pool_at, zb * NX + j] - dec_first
            limit = jnp.where((page >= 0) & (page < dec_count), live - page * span, 0)
            old_scores.append(
                jnp.where(lane < limit, scores[:, j * span : (j + 1) * span], NEG_FILL)
            )
    peak = new_scores
    for block in old_scores:
        peak = jnp.maximum(peak, block)
    peak = jnp.max(peak, axis=1, keepdims=True)
    new_weights = jnp.exp2((new_scores - peak) * FACTOR)
    weight_sum = new_weights
    answer = jnp.dot(
        new_weights.astype(BF16), new_page[1].astype(BF16), preferred_element_type=F32
    )
    for zb in range(nz):
        row_weights = [
            jnp.exp2((old_scores[zb * NX + j] - peak) * FACTOR) for j in range(NX)
        ]
        for block in row_weights:
            weight_sum = weight_sum + block
        answer = answer + jnp.dot(
            jnp.concatenate(row_weights, axis=1).astype(BF16),
            kv[zb * NX : (zb + 1) * NX, 1].reshape(NX * span, HD),
            preferred_element_type=F32,
        )
    answer = answer / jnp.sum(weight_sum, axis=1, keepdims=True)
    dec_rows[...] = jnp.where(holds == 1, answer, 0.0)
    dec_out[...] = jnp.zeros_like(dec_out)
    for h in range(REPEAT):
        dec_out[:steps, h * HD : (h + 1) * HD] = dec_rows[
            h * steps : (h + 1) * steps, :
        ].astype(BF16)
    pool_copy = remote(dec_out, dec_in, pool_send.at[0], pool_recv.at[0], pool=1 - pool_at)
    pool_copy.start()

    def block_at(k):
        both = jnp.minimum(z, nz - 1 - z)
        near = (k + 1) // 2
        paired = jnp.where(k % 2 == 1, z - near, z + near)
        beyond = jnp.where(z < nz // 2, z + k - both, z - k + both)
        return jnp.where(k <= 2 * both, paired, beyond)

    def core_copy(slot):
        return remote(
            core_out.at[slot], core_in.at[slot], core_send.at[slot], core_recv.at[slot], tp=sibling
        )

    def place_of(item):
        zb, s = block_at(item // 2), item % 2
        owner = zb // 2
        toward = 1 - 2 * s
        rank = ((y - owner) * toward + 2 * ny) % ny
        return zb, s, owner, toward, rank, owner * 2 + s

    def project(item):
        zb, s, _, _, _, slot = place_of(item)
        block = heads_out[zb, s]
        mine = zb % 2 == core

        @pl.when(mine)
        def _():
            for c in range(NX):
                stash[slot, c] = jnp.dot(block, weight[c], preferred_element_type=F32)

        @pl.when(jnp.logical_not(mine))
        def _():
            for c in range(NX):
                core_out[slot, c] = jnp.dot(
                    block, weight[c], preferred_element_type=F32
                ).astype(BF16)
            core_copy(slot).start()

    def y_copy(slot, dst, recv_sem, target):
        return remote(y_out.at[slot], dst, y_send.at[slot], recv_sem, tp=target * 2 + core)

    def pair_sum(item):
        zb, s, owner, toward, rank, slot = place_of(item)

        @pl.when(zb % 2 == core)
        def _():
            core_copy(slot).wait_recv()
            value = stash[slot] + core_in[slot].astype(F32)

            @pl.when(rank < 2)
            def _():
                stash[slot] = value

            @pl.when(rank >= 2)
            def _():
                y_out[slot] = value.astype(BF16)

            @pl.when(rank == 2)
            def _():
                y_copy(
                    slot, relay_in.at[s], relay_recv.at[s], (owner + toward + ny) % ny
                ).start()

            @pl.when(rank == 3)
            def _():
                y_copy(slot, owner_in.at[s, 1], owner_recv.at[s, 1], owner).start()

    def relay_sum(item):
        zb, s, owner, _, rank, slot = place_of(item)

        @pl.when((zb % 2 == core) & (rank == 1))
        def _():
            y_copy(slot, relay_in.at[s], relay_recv.at[s], y).wait_recv()
            y_out[slot] = (stash[slot] + relay_in[s].astype(F32)).astype(BF16)
            y_copy(slot, owner_in.at[s, 0], owner_recv.at[s, 0], owner).start()

    def advance(t, carry):
        z_step(t, 0)

        @pl.when((t >= 1) & (t <= W_PIECES // 2))
        def _():
            relay_weight(t - 1)

        return carry

    lax.fori_loop(1, 5, advance, 0)
    finish_weight()

    def item_step(item, carry):
        k = item // 2

        @pl.when((item % 2 == 0) & ((k == 2) | (k == 4) | (k == 7)))
        def _():
            z_step(jnp.where(k == 2, 5, jnp.where(k == 4, 6, 7)), 0)

        @pl.when(item < 2 * nz)
        def _():
            project(item)

        @pl.when((item >= 2) & (item < 2 * nz + 2))
        def _():
            pair_sum(item - 2)

        @pl.when((item >= 5) & (item < 2 * nz + 5))
        def _():
            relay_sum(item - 5)

        return carry

    lax.fori_loop(0, 2 * nz + 5, item_step, 0)

    def x_copy(s, distance):
        target = (x + distance) % NX
        return remote(
            x_out.at[s, target],
            x_in.at[x, s],
            x_send.at[s, distance],
            x_recv.at[s, distance],
            seq=z * NX + target,
        )

    load_r.wait()

    def finish(source, s, value):
        row = source * 2 * part + s * part
        out_ref[pl.ds(row, part), :] = (
            value.astype(F32) + resid[pl.ds(row, part), :].astype(F32)
        ).astype(BF16)

    for s in range(2):
        slot = y * 2 + s
        for n in range(2):
            y_copy(slot, owner_in.at[s, n], owner_recv.at[s, n], y).wait_recv()
        total = stash[slot] + owner_in[s, 0].astype(F32) + owner_in[s, 1].astype(F32)
        x_out[s] = total.astype(BF16)
        for distance in range(1, NX):
            x_copy(s, distance).start()
    for s in range(2):
        finish(x, s, x_out[s, x])
    for s in range(2):
        for distance in range(1, NX):
            source = (x + NX - distance) % NX
            remote(
                x_out.at[s, x],
                x_in.at[source, s],
                x_send.at[s, distance],
                x_recv.at[s, distance],
                seq=me,
            ).wait_recv()
            finish(source, s, x_in[source, s])

    pool_copy.wait()
    dec_ref[...] = dec_in[:steps, :]

    def drain(zb, carry):
        @pl.when((zb <= z) & (z < nz - 1))
        def _():
            kz_copy(zb, 0, me).wait_send()
            for s in range(2):
                az_copy(zb, s, 0, me).wait_send()

        @pl.when((zb >= z) & (z > 0))
        def _():
            kz_copy(zb, 1, me).wait_send()
            for s in range(2):
                az_copy(zb, s, 1, me).wait_send()

        kx_copy(zb, x, 0, right).wait_send()
        kx_copy(zb, x, 1, left).wait_send()
        kf_copy(zb, opposite, 0, right).wait_send()
        kf_copy(zb, opposite, 1, left).wait_send()

        for s in range(2):
            slot = (zb // 2) * 2 + s

            @pl.when(zb % 2 != core)
            def _():
                core_copy(slot).wait_send()

            @pl.when((zb % 2 == core) & (zb // 2 != y))
            def _():
                y_copy(slot, relay_in.at[s], relay_recv.at[s], y).wait_send()

        return carry

    lax.fori_loop(0, nz, drain, 0)
    for n in range(W_PIECES):
        wx_copy(x, n, 0, right).wait_send()
        wx_copy(x, n, 1, left).wait_send()
    for n in range(W_PIECES // 2):
        wf_copy(opposite, n, 0, right).wait_send()
        wf_copy(opposite, n, 1, left).wait_send()
    for s in range(2):
        for distance in range(1, NX):
            x_copy(s, distance).wait_send()


def per_device(
    q_pre,
    k_pre,
    v_pre,
    out_weight,
    residual,
    span_ids,
    page_counts,
    tail_rows,
    dest_group,
    dec_q,
    dec_k,
    dec_v,
):
    count = lax.axis_size("seq")
    nz = count // NX
    span, features = q_pre.shape[1:]
    depth, columns = out_weight.shape
    steps = dec_q.shape[2]
    part = span // 2
    pairs = REPEAT // 2
    dma = pltpu.SemaphoreType.DMA
    vmem, smem, hbm = (
        pl.BlockSpec(memory_space=space) for space in (pltpu.VMEM, pltpu.SMEM, pltpu.HBM)
    )
    tile = (NX, part, columns)
    mixed, decoded = pl.pallas_call(
        kernel,
        out_shape=(
            jax.ShapeDtypeStruct(residual.shape[1:], BF16),
            jax.ShapeDtypeStruct((steps, features), BF16),
        ),
        in_specs=[smem] * 4 + [vmem] * 3 + [hbm] * 5,
        out_specs=(vmem, vmem),
        scratch_shapes=[
            pltpu.VMEM((count, 2, span, HD), BF16),
            pltpu.VMEM((span, features), BF16),
            pltpu.VMEM((pairs, 2 * span, HD), BF16),
            pltpu.VMEM((pairs, 8, 2 * span), F32),
            pltpu.VMEM((pairs, 8, 2 * span), F32),
            pltpu.VMEM((pairs, HD, 2 * span), F32),
            pltpu.VMEM((nz, 2, part, features), BF16),
            pltpu.VMEM((NX, depth, columns), BF16),
            pltpu.VMEM(residual.shape[1:], BF16),
            pltpu.VMEM((nz,) + tile, BF16),
            pltpu.VMEM((nz,) + tile, BF16),
            pltpu.VMEM((nz,) + tile, F32),
            pltpu.VMEM((nz,) + tile, BF16),
            pltpu.VMEM((2,) + tile, BF16),
            pltpu.VMEM((2, 2) + tile, BF16),
            pltpu.VMEM((2,) + tile, BF16),
            pltpu.VMEM((NX, 2, part, columns), BF16),
            pltpu.VMEM((steps * REPEAT, HD), F32),
            pltpu.VMEM((2, span, HD), F32),
            pltpu.VMEM((16, features), BF16),
            pltpu.VMEM((16, features), BF16),
            dma((5,)),
            dma((2, nz)),
            dma((nz,)),
            dma((2, nz)),
            dma((2, nz)),
            dma((2, nz)),
            dma((2, nz)),
            dma((2, W_PIECES)),
            dma((2, W_PIECES)),
            dma((2, W_PIECES // 2)),
            dma((2, W_PIECES // 2)),
            dma((2, nz, 2)),
            dma((nz, 2)),
            dma((nz,)),
            dma((nz,)),
            dma((nz,)),
            dma((2,)),
            dma((2, 2)),
            dma((2, NX)),
            dma((2, NX)),
            dma((1,)),
            dma((1,)),
        ],
        compiler_params=pltpu.CompilerParams(
            collective_id=0, has_side_effects=True, vmem_limit_bytes=48 << 20
        ),
    )(
        span_ids,
        page_counts,
        tail_rows,
        dest_group,
        dec_q,
        dec_k,
        dec_v,
        k_pre[0],
        v_pre[0],
        q_pre[0],
        out_weight,
        residual[0],
    )
    return (mixed[None], decoded[None, None])


def solution(mesh):
    placed = (
        P("pool", "seq", "tp"),
        P("pool", "seq", "tp"),
        P("pool", "seq", "tp"),
        P("tp", "seq"),
        P("pool", "tp", "seq"),
        P(),
        P(),
        P(),
        P(),
        P(None, None, None, "tp"),
        P(None, None, None, "tp"),
        P(None, None, None, "tp"),
    )
    return jax.shard_map(
        per_device,
        mesh=mesh,
        in_specs=placed,
        out_specs=(P("pool", "tp", "seq"), P("pool", "seq", None, "tp")),
        check_vma=False,
    )
```

```python
import math

import jax
import jax.numpy as jnp
from jax import lax
from jax.experimental import pallas as pl
from jax.experimental.pallas import tpu as pltpu
from jax.sharding import PartitionSpec as P

HD = 128
QH = 64
KVH = 8
REPEAT = QH // KVH
NX = 4
NEG_FILL = -1e30
FAR_FILL = 1e30
FACTOR = math.log2(math.e) / math.sqrt(HD)
MESH = pl.DeviceIdType.MESH
F32 = jnp.float32
BF16 = jnp.bfloat16
W_PIECES = 4
W_START = 8
W_RELAY = 1
RELAY_LAG = 8
OWNER_LAG = 12


def unit(block, *turns):
    return [block * 4 + turn for turn in turns]


SEGMENTS = [
    unit(0, 0),
    unit(1, 0),
    unit(2, 0),
    unit(3, 0) + unit(0, 1, 2) + unit(1, 1, 2),
    unit(4, 0) + unit(2, 1, 2) + unit(3, 1, 2) + unit(4, 1, 2),
    unit(5, 0, 1, 2) + unit(0, 3) + unit(1, 3) + unit(2, 3) + unit(3, 3) + unit(4, 3),
    unit(5, 3) + unit(6, 3, 1, 2, 0),
    unit(7, 3, 1, 2, 0),
]
UNITS = sum(SEGMENTS, [])
STEP_AT = [sum(len(segment) for segment in SEGMENTS[:t]) for t in range(len(SEGMENTS))]
NEAR_AT = UNITS.index(1)
FAR_AT = UNITS.index(3)


def matmul_nt(a, b):
    return lax.dot_general(a, b, (((1,), (1,)), ((), ())), preferred_element_type=F32)


def matmul_tn(a, b):
    return lax.dot_general(a, b, (((0,), (0,)), ((), ())), preferred_element_type=F32)


def remote(src, dst, send_sem, recv_sem, **target):
    return pltpu.make_async_remote_copy(
        src_ref=src,
        dst_ref=dst,
        send_sem=send_sem,
        recv_sem=recv_sem,
        device_id=target,
        device_id_type=MESH,
    )


def kernel(
    span_ref,
    counts_ref,
    tails_ref,
    dest_ref,
    dq_hbm,
    dk_hbm,
    dv_hbm,
    k_hbm,
    v_hbm,
    q_hbm,
    w_hbm,
    res_hbm,
    out_ref,
    dec_ref,
    dq_ref,
    dk_ref,
    dv_ref,
    kv,
    q_in,
    rows_of,
    high_of,
    total_of,
    accum,
    heads_out,
    weight,
    resid,
    core_out,
    core_in,
    stash,
    y_out,
    relay_in,
    owner_in,
    x_out,
    x_in,
    dec_rows,
    new_page,
    dec_out,
    dec_in,
    local_sem,
    kz_send,
    kz_recv,
    kx_send,
    kx_recv,
    kf_send,
    kf_recv,
    wx_send,
    wx_recv,
    wf_send,
    wf_recv,
    az_send,
    az_recv,
    core_send,
    core_recv,
    y_send,
    relay_recv,
    owner_recv,
    x_send,
    x_recv,
    pool_send,
    pool_recv,
):
    me = lax.axis_index("seq")
    tp_at = lax.axis_index("tp")
    pool_at = lax.axis_index("pool")
    nz = kv.shape[0] // NX
    ny = NX
    span = kv.shape[2]
    z, x = me // NX, me % NX
    y, core = tp_at // 2, tp_at % 2
    right, left = z * NX + (x + 1) % NX, z * NX + (x + 3) % NX
    opposite = (x + 2) % NX
    sibling = tp_at + 1 - 2 * core
    part = heads_out.shape[2]
    steps = dec_ref.shape[0]
    requests = counts_ref.shape[1]

    load_k = pltpu.make_async_copy(k_hbm, kv.at[me, 0], local_sem.at[0])
    load_v = pltpu.make_async_copy(v_hbm, kv.at[me, 1], local_sem.at[1])
    load_q = pltpu.make_async_copy(q_hbm, q_in, local_sem.at[2])
    load_w = pltpu.make_async_copy(w_hbm, weight.at[x], local_sem.at[3])
    load_r = pltpu.make_async_copy(res_hbm, resid, local_sem.at[4])
    load_dec = [
        pltpu.make_async_copy(src, dst, local_sem.at[5 + n])
        for n, (src, dst) in enumerate(((dq_hbm, dq_ref), (dk_hbm, dk_ref), (dv_hbm, dv_ref)))
    ]
    for load in (load_k, load_v, load_q, load_w, load_r, *load_dec):
        load.start()

    barrier = pltpu.get_barrier_semaphore()

    def greet(**target):
        pl.semaphore_signal(barrier, inc=1, device_id=target, device_id_type=MESH)

    for distance in range(1, NX):
        greet(seq=z * NX + (x + distance) % NX)
        greet(tp=((y + distance) % ny) * 2 + core)
    greet(tp=sibling)
    greet(pool=1 - pool_at)

    @pl.when(z > 0)
    def _():
        greet(seq=me - NX)

    @pl.when(z < nz - 1)
    def _():
        greet(seq=me + NX)

    load_k.wait()
    load_v.wait()
    pl.semaphore_wait(barrier, 8 + jnp.where(z > 0, 1, 0) + jnp.where(z < nz - 1, 1, 0))

    def kz_copy(zb, which, direction, target):
        slot = kv.at[zb * NX + x, which]
        return remote(
            slot, slot, kz_send.at[direction, zb, which], kz_recv.at[zb, which], seq=target
        )

    def kx_copy(zb, xb, direction, target):
        slot = kv.at[zb * NX + xb]
        return remote(
            slot, slot, kx_send.at[direction, zb], kx_recv.at[direction, zb], seq=target
        )

    def kf_copy(zb, xb, direction, target):
        slot = kv.at[zb * NX + xb, direction]
        return remote(
            slot, slot, kf_send.at[direction, zb], kf_recv.at[direction, zb], seq=target
        )

    def spread(zb):
        kx_copy(zb, x, 0, right).start()
        kx_copy(zb, x, 1, left).start()

    def relay(zb):
        kx_copy(zb, (x + 3) % NX, 0, right).wait_recv()
        kf_copy(zb, (x + 3) % NX, 0, right).start()
        kx_copy(zb, (x + 1) % NX, 1, left).wait_recv()
        kf_copy(zb, (x + 1) % NX, 1, left).start()

    height = weight.shape[1] // W_PIECES

    def w_piece(xb, piece):
        return weight.at[xb, pl.ds(piece * height, height)]

    def wx_copy(xb, piece, direction, target):
        slot = w_piece(xb, piece)
        return remote(
            slot, slot, wx_send.at[direction, piece], wx_recv.at[direction, piece], seq=target
        )

    def wf_copy(xb, n, direction, target):
        slot = w_piece(xb, direction * (W_PIECES // 2) + n)
        return remote(
            slot, slot, wf_send.at[direction, n], wf_recv.at[direction, n], seq=target
        )

    def spread_weight():
        load_w.wait()
        for n in range(W_PIECES):
            wx_copy(x, n, 0, right).start()
            wx_copy(x, (n + W_PIECES // 2) % W_PIECES, 1, left).start()

    def relay_weight(n):
        wx_copy((x + 3) % NX, n, 0, right).wait_recv()
        wf_copy((x + 3) % NX, n, 0, right).start()
        wx_copy((x + 1) % NX, n + W_PIECES // 2, 1, left).wait_recv()
        wf_copy((x + 1) % NX, n, 1, left).start()

    def finish_near():
        for n in range(W_PIECES // 2):
            wx_copy((x + 3) % NX, n + W_PIECES // 2, 0, right).wait_recv()
            wx_copy((x + 1) % NX, n, 1, left).wait_recv()

    def finish_far():
        for n in range(W_PIECES // 2):
            wf_copy(opposite, n, 0, right).wait_recv()
            wf_copy(opposite, n, 1, left).wait_recv()

    own = span_ref[pool_at, me]
    begin = jnp.int32(0)
    first = jnp.int32(0)
    dec_first, dec_count, dec_tail, dec_no, holds = (jnp.int32(0),) * 5
    for r in range(requests):
        count = counts_ref[pool_at, r]
        first = jnp.where(begin <= own, begin, first)
        match = dest_ref[pool_at, r] == me
        dec_first = jnp.where(match, begin, dec_first)
        dec_count = jnp.where(match, count, dec_count)
        dec_tail = jnp.where(match, tails_ref[pool_at, r], dec_tail)
        dec_no = jnp.where(match, r, dec_no)
        holds = jnp.where(match, 1, holds)
        begin = begin + count

    width = 2 * HD

    def attend(zb, diagonal):
        keys = kv[pl.ds(zb * NX, NX), 0].reshape(NX * span, HD)
        values = kv[pl.ds(zb * NX, NX), 1].reshape(NX * span, HD)
        pages = [span_ref[pool_at, zb * NX + j] for j in range(NX)]
        if diagonal:
            ahead = lax.broadcasted_iota(jnp.int32, (span, width), 0) - (
                lax.broadcasted_iota(jnp.int32, (span, width), 1) % span
            )
        for pair in range(REPEAT // 2):
            scores = matmul_nt(keys, rows_of[pair])
            blocks = [scores[j * span : (j + 1) * span] for j in range(NX)]
            if diagonal:
                blocks = [
                    jnp.where(
                        ahead <= jnp.where(page >= first, (own - page) * span, -2 * span),
                        block,
                        NEG_FILL,
                    )
                    for page, block in zip(pages, blocks)
                ]
                peaks = [jnp.max(block, axis=0, keepdims=True) for block in blocks]
            else:
                seen = [(page >= first) & (page < own) for page in pages]
                peaks = [
                    jnp.where(is_seen, jnp.max(block, axis=0, keepdims=True), NEG_FILL)
                    for is_seen, block in zip(seen, blocks)
                ]
            new_high = jnp.maximum(
                jnp.maximum(peaks[0], peaks[1]), jnp.maximum(peaks[2], peaks[3])
            )
            if not diagonal:
                old_high = high_of[pair, 0:1]
                new_high = jnp.maximum(new_high, old_high)
            weights = []
            sums = []
            for j, block in enumerate(blocks):
                base = new_high if diagonal else jnp.where(seen[j], new_high, FAR_FILL)
                weights.append(jnp.exp2((block - base) * FACTOR))
                sums.append(jnp.sum(weights[-1], axis=0, keepdims=True))
            total = (sums[0] + sums[1]) + (sums[2] + sums[3])
            update = matmul_tn(values, jnp.concatenate(weights, axis=0).astype(BF16))
            if not diagonal:
                fade = jnp.exp2((old_high - new_high) * FACTOR)
                total = total + total_of[pair, 0:1] * fade
                update = update + accum[pair] * fade
            high_of[pair, 0:1] = new_high
            total_of[pair, 0:1] = total
            accum[pair] = update

    lag = 1 + jnp.where((z > 0) & (z < nz - 1), 1, 0) + jnp.where((z > 1) & (z < nz - 2), 1, 0)

    load_q.wait()
    for pair in range(REPEAT // 2):
        for n in range(2):
            h = 2 * pair + n
            rows_of[pair, n * span : (n + 1) * span, :] = q_in[:, h * HD : (h + 1) * HD]

    def far_wait(zb):
        kf_copy(zb, opposite, 0, right).wait_recv()
        kf_copy(zb, opposite, 1, left).wait_recv()

    def gather_step(t, carry):
        low, high = z - t, z + t

        for which in range(2):

            @pl.when((t > 0) & (low >= 0))
            def _():
                kz_copy(low, which, 0, me).wait_recv()

            @pl.when((low >= 0) & (z < nz - 1))
            def _():
                kz_copy(low, which, 0, me + NX).start()

            @pl.when((t > 0) & (high < nz))
            def _():
                kz_copy(high, which, 1, me).wait_recv()

            @pl.when((high < nz) & (z > 0))
            def _():
                kz_copy(high, which, 1, me - NX).start()

        @pl.when(low >= 0)
        def _():
            spread(low)

        @pl.when((t > 0) & (high < nz))
        def _():
            spread(high)

        past = t - lag

        @pl.when((past >= 0) & (z - past >= 0))
        def _():
            relay(z - past)

        @pl.when((past > 0) & (z + past < nz))
        def _():
            relay(z + past)

        @pl.when(t == W_START)
        def _():
            spread_weight()

        ready = t - lag - 2

        @pl.when(ready == 0)
        def _():
            far_wait(z)
            attend(z, True)

        for sign in (-1, 1):
            zb = z + sign * ready

            @pl.when((ready > 0) & (zb >= 0) & (zb < nz))
            def _():
                far_wait(zb)
                attend(zb, False)

        return carry

    lax.fori_loop(0, nz + 3, gather_step, 0)

    for pair in range(REPEAT // 2):
        result = accum[pair] / total_of[pair, 0:1]
        for n in range(2):
            h = 2 * pair + n
            block = jnp.transpose(result[:, n * span : (n + 1) * span]).astype(BF16)
            for s in range(2):
                heads_out[z, s, :, h * HD : (h + 1) * HD] = block[s * part : (s + 1) * part]

    def az_copy(zb, s, direction, target):
        slot = heads_out.at[zb, s]
        return remote(slot, slot, az_send.at[direction, zb, s], az_recv.at[zb, s], seq=target)

    def z_step(t, carry):
        low, high = z - t, z + t
        for s in range(2):

            @pl.when((t > 0) & (low >= 0))
            def _():
                az_copy(low, s, 0, me).wait_recv()

            @pl.when((low >= 0) & (z < nz - 1))
            def _():
                az_copy(low, s, 0, me + NX).start()

            @pl.when((t > 0) & (high < nz))
            def _():
                az_copy(high, s, 1, me).wait_recv()

            @pl.when((high < nz) & (z > 0))
            def _():
                az_copy(high, s, 1, me - NX).start()

        return carry

    z_step(0, 0)

    for load in load_dec:
        load.wait()
    queries = dq_ref[pool_at, dec_no].astype(F32)
    for h in range(REPEAT):
        dec_rows[h * steps : (h + 1) * steps, :] = queries[:, h * HD : (h + 1) * HD]
    rows = dec_rows[...].astype(BF16)
    new_page[...] = jnp.zeros_like(new_page)
    new_page[0, :steps, :] = dk_ref[pool_at, dec_no].astype(F32)
    new_page[1, :steps, :] = dv_ref[pool_at, dec_no].astype(F32)
    row_count = rows.shape[0]
    lane = lax.broadcasted_iota(jnp.int32, (row_count, span), 1)
    step_of = lax.broadcasted_iota(jnp.int32, (row_count, span), 0) % steps
    new_scores = jnp.where(
        lane <= step_of, matmul_nt(rows, new_page[0].astype(BF16)), NEG_FILL
    )
    live = (dec_count - 1) * span + dec_tail
    old_scores = []
    for zb in range(nz):
        keys = kv[zb * NX : (zb + 1) * NX, 0].reshape(NX * span, HD)
        scores = matmul_nt(rows, keys)
        for j in range(NX):
            page = span_ref[pool_at, zb * NX + j] - dec_first
            limit = jnp.where((page >= 0) & (page < dec_count), live - page * span, 0)
            old_scores.append(
                jnp.where(lane < limit, scores[:, j * span : (j + 1) * span], NEG_FILL)
            )
    peak = new_scores
    for block in old_scores:
        peak = jnp.maximum(peak, block)
    peak = jnp.max(peak, axis=1, keepdims=True)
    new_weights = jnp.exp2((new_scores - peak) * FACTOR)
    weight_sum = new_weights
    answer = jnp.dot(
        new_weights.astype(BF16), new_page[1].astype(BF16), preferred_element_type=F32
    )
    for zb in range(nz):
        row_weights = [
            jnp.exp2((old_scores[zb * NX + j] - peak) * FACTOR) for j in range(NX)
        ]
        for block in row_weights:
            weight_sum = weight_sum + block
        answer = answer + jnp.dot(
            jnp.concatenate(row_weights, axis=1).astype(BF16),
            kv[zb * NX : (zb + 1) * NX, 1].reshape(NX * span, HD),
            preferred_element_type=F32,
        )
    answer = answer / jnp.sum(weight_sum, axis=1, keepdims=True)
    dec_rows[...] = jnp.where(holds == 1, answer, 0.0)
    dec_out[...] = jnp.zeros_like(dec_out)
    for h in range(REPEAT):
        dec_out[:steps, h * HD : (h + 1) * HD] = dec_rows[
            h * steps : (h + 1) * steps, :
        ].astype(BF16)
    pool_copy = remote(dec_out, dec_in, pool_send.at[0], pool_recv.at[0], pool=1 - pool_at)
    pool_copy.start()

    edge = jnp.minimum(z, nz - 1 - z)

    def look_up(table, index):
        value = jnp.int32(table[-1])
        for n in reversed(range(len(table) - 1)):
            value = jnp.where(index <= n, table[n], value)
        return value

    def place_of(unit):
        code = look_up(UNITS, unit)
        k, turn = code // 4, code % 4
        near = (k + 1) // 2
        paired = jnp.where(k % 2 == 1, z - near, z + near)
        beyond = jnp.where(z < nz // 2, z + k - edge, z - k + edge)
        zb = jnp.where(k <= 2 * edge, paired, beyond)
        quarter = (x + jnp.where(turn == 1, 3, jnp.where(turn == 2, 1, jnp.where(turn == 3, 2, 0)))) % NX
        owner = zb // 2
        toward = 1 - 2 * (quarter % 2)
        rank = ((y - owner) * toward + 2 * ny) % ny
        return zb % 2 == core, zb, quarter, owner, toward, rank, owner * NX + quarter

    def core_copy(slot):
        return remote(
            core_out.at[slot], core_in.at[slot], core_send.at[slot], core_recv.at[slot], tp=sibling
        )

    def project(unit):
        mine, zb, quarter, _, _, _, slot = place_of(unit)
        block = heads_out[zb].reshape(span, heads_out.shape[3])
        product = jnp.dot(block, weight[quarter], preferred_element_type=F32)

        @pl.when(mine)
        def _():
            stash[slot] = product

        @pl.when(jnp.logical_not(mine))
        def _():
            core_out[slot] = product.astype(BF16)
            core_copy(slot).start()

    def y_copy(slot, dst, recv_sem, target):
        return remote(y_out.at[slot], dst, y_send.at[slot], recv_sem, tp=target * 2 + core)

    def pair_sum(unit, carry):
        mine, _, quarter, owner, toward, rank, slot = place_of(unit)

        @pl.when(mine)
        def _():
            core_copy(slot).wait_recv()
            value = stash[slot] + core_in[slot].astype(F32)

            @pl.when(rank < 2)
            def _():
                stash[slot] = value

            @pl.when(rank >= 2)
            def _():
                y_out[slot] = value.astype(BF16)

            @pl.when(rank == 2)
            def _():
                y_copy(
                    slot, relay_in.at[quarter], relay_recv.at[quarter], (owner + toward + ny) % ny
                ).start()

            @pl.when(rank == 3)
            def _():
                y_copy(
                    slot, owner_in.at[quarter, 1], owner_recv.at[quarter, 1], owner
                ).start()

        return carry

    def relay_sum(unit, carry):
        mine, _, quarter, owner, _, rank, slot = place_of(unit)

        @pl.when(mine & (rank == 1))
        def _():
            y_copy(slot, relay_in.at[quarter], relay_recv.at[quarter], y).wait_recv()
            y_out[slot] = (stash[slot] + relay_in[quarter].astype(F32)).astype(BF16)
            y_copy(slot, owner_in.at[quarter, 0], owner_recv.at[quarter, 0], owner).start()

        return carry

    def x_copy(quarter, source, target):
        distance = (target + NX - source) % NX
        return remote(
            x_out.at[quarter],
            x_in.at[source],
            x_send.at[distance],
            x_recv.at[distance],
            seq=z * NX + target,
        )

    def finish(source, value):
        row = pl.ds(source * span, span)
        out_ref[row, :] = (value.astype(F32) + resid[row, :].astype(F32)).astype(BF16)

    def owner_sum(unit, carry):
        mine, _, quarter, _, _, rank, slot = place_of(unit)

        @pl.when(mine & (rank == 0))
        def _():
            for n in range(2):
                y_copy(slot, owner_in.at[quarter, n], owner_recv.at[quarter, n], y).wait_recv()
            total = (
                stash[slot]
                + owner_in[quarter, 0].astype(F32)
                + owner_in[quarter, 1].astype(F32)
            )

            @pl.when(quarter == x)
            def _():
                finish(x, total)

            @pl.when(quarter != x)
            def _():
                x_out[quarter] = total.astype(BF16)
                x_copy(quarter, x, quarter).start()

        return carry

    count = len(UNITS)

    def clipped(value):
        return jnp.clip(value, 0, count)

    def flushing(unit):
        return (unit >= count) | ((edge == 0) & ((unit == STEP_AT[6]) | (unit == STEP_AT[7])))

    def pairs_by(unit):
        return clipped(jnp.where(unit >= count, unit, unit - 1 + jnp.where(flushing(unit), 1, 0)))

    def relays_by(unit):
        late = jnp.where(unit >= STEP_AT[7], count - 4 + unit - count, unit - RELAY_LAG)
        return clipped(late)

    def owners_by(unit):
        late = jnp.where(unit > count, count - 5 + unit - count, unit - OWNER_LAG)
        return clipped(late)

    def steps_by(unit):
        done = jnp.int32(0)
        for t in range(1, nz):
            at = jnp.int32(STEP_AT[t])
            if t == 5:
                at = at - jnp.where((edge == 1) | (edge == 2), 2, 0)
            if t == 6:
                at = at - jnp.where(edge == 1, 2, 0)
            done = done + jnp.where(unit >= at, 1, 0)
        return done

    def advance(t, carry):
        z_step(t, 0)

        @pl.when((t >= W_RELAY) & (t < W_RELAY + W_PIECES // 2))
        def _():
            relay_weight(t - W_RELAY)

        return carry

    def unit_step(unit, carry):
        lax.fori_loop(pairs_by(unit - 1), pairs_by(unit), pair_sum, 0)
        lax.fori_loop(relays_by(unit - 1), relays_by(unit), relay_sum, 0)
        lax.fori_loop(owners_by(unit - 1), owners_by(unit), owner_sum, 0)
        lax.fori_loop(steps_by(unit - 1) + 1, steps_by(unit) + 1, advance, 0)

        @pl.when(unit == NEAR_AT)
        def _():
            finish_near()

        @pl.when(unit == FAR_AT)
        def _():
            finish_far()

        @pl.when(unit < count)
        def _():
            project(unit)

        return carry

    load_r.wait()
    lax.fori_loop(0, count + 6, unit_step, 0)

    for distance in range(1, NX):
        source = (x + NX - distance) % NX
        x_copy(x, source, x).wait_recv()
        finish(source, x_in[source])

    pool_copy.wait()
    dec_ref[...] = dec_in[:steps, :]

    def drain(zb, carry):
        @pl.when((zb <= z) & (z < nz - 1))
        def _():
            for s in range(2):
                kz_copy(zb, s, 0, me).wait_send()
                az_copy(zb, s, 0, me).wait_send()

        @pl.when((zb >= z) & (z > 0))
        def _():
            for s in range(2):
                kz_copy(zb, s, 1, me).wait_send()
                az_copy(zb, s, 1, me).wait_send()

        kx_copy(zb, x, 0, right).wait_send()
        kx_copy(zb, x, 1, left).wait_send()
        kf_copy(zb, opposite, 0, right).wait_send()
        kf_copy(zb, opposite, 1, left).wait_send()

        for quarter in range(NX):
            slot = (zb // 2) * NX + quarter

            @pl.when(zb % 2 != core)
            def _():
                core_copy(slot).wait_send()

            @pl.when((zb % 2 == core) & (zb // 2 != y))
            def _():
                y_copy(slot, relay_in.at[quarter], relay_recv.at[quarter], y).wait_send()

        return carry

    lax.fori_loop(0, nz, drain, 0)
    for n in range(W_PIECES):
        wx_copy(x, n, 0, right).wait_send()
        wx_copy(x, n, 1, left).wait_send()
    for n in range(W_PIECES // 2):
        wf_copy(opposite, n, 0, right).wait_send()
        wf_copy(opposite, n, 1, left).wait_send()
    for distance in range(1, NX):
        target = (x + distance) % NX
        x_copy(target, x, target).wait_send()


def per_device(
    q_pre,
    k_pre,
    v_pre,
    out_weight,
    residual,
    span_ids,
    page_counts,
    tail_rows,
    dest_group,
    dec_q,
    dec_k,
    dec_v,
):
    count = lax.axis_size("seq")
    nz = count // NX
    span, features = q_pre.shape[1:]
    depth, columns = out_weight.shape
    steps = dec_q.shape[2]
    part = span // 2
    slots = nz // 2 * NX
    pairs = REPEAT // 2
    dma = pltpu.SemaphoreType.DMA
    vmem, smem, hbm = (
        pl.BlockSpec(memory_space=space) for space in (pltpu.VMEM, pltpu.SMEM, pltpu.HBM)
    )
    tile = (span, columns)
    mixed, decoded = pl.pallas_call(
        kernel,
        out_shape=(
            jax.ShapeDtypeStruct(residual.shape[1:], BF16),
            jax.ShapeDtypeStruct((steps, features), BF16),
        ),
        in_specs=[smem] * 4 + [hbm] * 8,
        out_specs=(vmem, vmem),
        scratch_shapes=[
            pltpu.VMEM(dec_q.shape, BF16),
            pltpu.VMEM(dec_k.shape, BF16),
            pltpu.VMEM(dec_v.shape, BF16),
            pltpu.VMEM((count, 2, span, HD), BF16),
            pltpu.VMEM((span, features), BF16),
            pltpu.VMEM((pairs, 2 * span, HD), BF16),
            pltpu.VMEM((pairs, 8, 2 * span), F32),
            pltpu.VMEM((pairs, 8, 2 * span), F32),
            pltpu.VMEM((pairs, HD, 2 * span), F32),
            pltpu.VMEM((nz, 2, part, features), BF16),
            pltpu.VMEM((NX, depth, columns), BF16),
            pltpu.VMEM(residual.shape[1:], BF16),
            pltpu.VMEM((slots,) + tile, BF16),
            pltpu.VMEM((slots,) + tile, BF16),
            pltpu.VMEM((slots,) + tile, F32),
            pltpu.VMEM((slots,) + tile, BF16),
            pltpu.VMEM((NX,) + tile, BF16),
            pltpu.VMEM((NX, 2) + tile, BF16),
            pltpu.VMEM((NX,) + tile, BF16),
            pltpu.VMEM((NX,) + tile, BF16),
            pltpu.VMEM((steps * REPEAT, HD), F32),
            pltpu.VMEM((2, span, HD), F32),
            pltpu.VMEM((16, features), BF16),
            pltpu.VMEM((16, features), BF16),
            dma((8,)),
            dma((2, nz, 2)),
            dma((nz, 2)),
            dma((2, nz)),
            dma((2, nz)),
            dma((2, nz)),
            dma((2, nz)),
            dma((2, W_PIECES)),
            dma((2, W_PIECES)),
            dma((2, W_PIECES // 2)),
            dma((2, W_PIECES // 2)),
            dma((2, nz, 2)),
            dma((nz, 2)),
            dma((slots,)),
            dma((slots,)),
            dma((slots,)),
            dma((NX,)),
            dma((NX, 2)),
            dma((NX,)),
            dma((NX,)),
            dma((1,)),
            dma((1,)),
        ],
        compiler_params=pltpu.CompilerParams(
            collective_id=0, has_side_effects=True, vmem_limit_bytes=60 << 20
        ),
    )(
        span_ids,
        page_counts,
        tail_rows,
        dest_group,
        dec_q,
        dec_k,
        dec_v,
        k_pre[0],
        v_pre[0],
        q_pre[0],
        out_weight,
        residual[0],
    )
    return (mixed[None], decoded[None, None])


def solution(mesh):
    placed = (
        P("pool", "seq", "tp"),
        P("pool", "seq", "tp"),
        P("pool", "seq", "tp"),
        P("tp", "seq"),
        P("pool", "tp", "seq"),
        P(),
        P(),
        P(),
        P(),
        P(None, None, None, "tp"),
        P(None, None, None, "tp"),
        P(None, None, None, "tp"),
    )
    return jax.shard_map(
        per_device,
        mesh=mesh,
        in_specs=placed,
        out_specs=(P("pool", "tp", "seq"), P("pool", "seq", None, "tp")),
        check_vma=False,
    )
```

```python
import math

import jax
import jax.numpy as jnp
from jax import lax
from jax.experimental import pallas as pl
from jax.experimental.pallas import tpu as pltpu
from jax.sharding import PartitionSpec as P

HD = 128
QH = 64
KVH = 8
REPEAT = QH // KVH
NX = 4
NEG_FILL = -1e30
FAR_FILL = 1e30
FACTOR = math.log2(math.e) / math.sqrt(HD)
MESH = pl.DeviceIdType.MESH
F32 = jnp.float32
BF16 = jnp.bfloat16
W_PIECES = 4
W_START = 8
PAIR_LAG = 2
RELAY_LAG = 8
OWNER_LAG = 12


def unit(block, *turns):
    return [block * 4 + turn for turn in turns]


SEGMENTS = [
    unit(0, 0),
    unit(1, 0),
    unit(2, 0) + unit(0, 1, 2) + unit(1, 1, 2),
    unit(3, 0) + unit(2, 1, 2) + unit(3, 1, 2),
    unit(0, 3) + unit(4, 0, 1) + unit(1, 3) + unit(4, 2) + unit(2, 3) + unit(3, 3) + unit(4, 3),
    unit(5, 3, 1, 2, 0),
    unit(6, 3, 1, 2, 0),
    unit(7, 3, 1, 2, 0),
]
UNITS = sum(SEGMENTS, [])
STEP_AT = [sum(len(segment) for segment in SEGMENTS[:t]) for t in range(len(SEGMENTS))]
NEAR_AT = UNITS.index(1)
FAR_AT = UNITS.index(3)


def matmul_nt(a, b):
    return lax.dot_general(a, b, (((1,), (1,)), ((), ())), preferred_element_type=F32)


def remote(src, dst, send_sem, recv_sem, **target):
    return pltpu.make_async_remote_copy(
        src_ref=src,
        dst_ref=dst,
        send_sem=send_sem,
        recv_sem=recv_sem,
        device_id=target,
        device_id_type=MESH,
    )


def kernel(
    span_ref,
    counts_ref,
    tails_ref,
    dest_ref,
    dq_hbm,
    dk_hbm,
    dv_hbm,
    k_hbm,
    v_hbm,
    q_hbm,
    w_hbm,
    res_hbm,
    out_ref,
    dec_ref,
    dq_ref,
    dk_ref,
    dv_ref,
    kv,
    q_in,
    rows_of,
    high_of,
    total_of,
    accum,
    heads_out,
    weight,
    resid,
    core_out,
    core_in,
    stash,
    y_out,
    relay_in,
    owner_in,
    x_out,
    x_in,
    dec_rows,
    new_page,
    dec_out,
    dec_in,
    local_sem,
    kz_send,
    kz_recv,
    kx_send,
    kx_recv,
    kf_send,
    kf_recv,
    wx_send,
    wx_recv,
    wf_send,
    wf_recv,
    az_send,
    az_recv,
    core_send,
    core_recv,
    y_send,
    relay_recv,
    owner_recv,
    x_send,
    x_recv,
    pool_send,
    pool_recv,
):
    me = lax.axis_index("seq")
    tp_at = lax.axis_index("tp")
    pool_at = lax.axis_index("pool")
    nz = kv.shape[0] // NX
    ny = NX
    span = kv.shape[2]
    z, x = me // NX, me % NX
    y, core = tp_at // 2, tp_at % 2
    right, left = z * NX + (x + 1) % NX, z * NX + (x + 3) % NX
    opposite = (x + 2) % NX
    sibling = tp_at + 1 - 2 * core
    part = heads_out.shape[2]
    steps = dec_ref.shape[0]
    requests = counts_ref.shape[1]

    load_k = pltpu.make_async_copy(k_hbm, kv.at[me, 0], local_sem.at[0])
    load_v = pltpu.make_async_copy(v_hbm, kv.at[me, 1], local_sem.at[1])
    load_q = pltpu.make_async_copy(q_hbm, q_in, local_sem.at[2])
    load_w = pltpu.make_async_copy(w_hbm, weight.at[x], local_sem.at[3])
    load_r = pltpu.make_async_copy(res_hbm, resid, local_sem.at[4])
    load_dec = [
        pltpu.make_async_copy(src, dst, local_sem.at[5 + n])
        for n, (src, dst) in enumerate(((dq_hbm, dq_ref), (dk_hbm, dk_ref), (dv_hbm, dv_ref)))
    ]
    for load in (load_k, load_v, load_q, load_w, load_r, *load_dec):
        load.start()

    barrier = pltpu.get_barrier_semaphore()

    def greet(**target):
        pl.semaphore_signal(barrier, inc=1, device_id=target, device_id_type=MESH)

    for distance in range(1, NX):
        greet(seq=z * NX + (x + distance) % NX)
        greet(tp=((y + distance) % ny) * 2 + core)
    greet(tp=sibling)
    greet(pool=1 - pool_at)

    around = 0
    for distance in (1, 2):
        for sign in (-1, 1):
            there = (z + sign * distance >= 0) & (z + sign * distance < nz)
            around = around + jnp.where(there, 1, 0)

            @pl.when(there)
            def _():
                greet(seq=me + sign * distance * NX)

    load_k.wait()
    load_v.wait()
    pl.semaphore_wait(barrier, 8 + around)

    def kz_copy(zb, which, direction, distance):
        slot = kv.at[zb * NX + x, which]
        return remote(
            slot,
            slot,
            kz_send.at[direction, zb, which * 2 + distance - 1],
            kz_recv.at[zb, which],
            seq=me + (1 - 2 * direction) * distance * NX,
        )

    def kz_sends(zb, direction, act):
        travelled = (z - zb) * (1 - 2 * direction)
        for which in range(2):
            for distance in (1, 2):
                target = z + (1 - 2 * direction) * distance

                @pl.when(
                    (travelled >= 0) & ((travelled & 1) == 0) & (target >= 0) & (target < nz)
                )
                def _():
                    act(kz_copy(zb, which, direction, distance))

    def kx_copy(zb, xb, direction, target):
        slot = kv.at[zb * NX + xb]
        return remote(
            slot, slot, kx_send.at[direction, zb], kx_recv.at[direction, zb], seq=target
        )

    def kf_copy(zb, xb, direction, target):
        slot = kv.at[zb * NX + xb, direction]
        return remote(
            slot, slot, kf_send.at[direction, zb], kf_recv.at[direction, zb], seq=target
        )

    def spread(zb):
        kx_copy(zb, x, 0, right).start()
        kx_copy(zb, x, 1, left).start()

    def relay(zb):
        kx_copy(zb, (x + 3) % NX, 0, right).wait_recv()
        kf_copy(zb, (x + 3) % NX, 0, right).start()
        kx_copy(zb, (x + 1) % NX, 1, left).wait_recv()
        kf_copy(zb, (x + 1) % NX, 1, left).start()

    height = weight.shape[1] // W_PIECES

    def w_piece(xb, piece):
        return weight.at[xb, pl.ds(piece * height, height)]

    def wx_copy(xb, piece, direction, target):
        slot = w_piece(xb, piece)
        return remote(
            slot, slot, wx_send.at[direction, piece], wx_recv.at[direction, piece], seq=target
        )

    def wf_copy(xb, n, direction, target):
        slot = w_piece(xb, direction * (W_PIECES // 2) + n)
        return remote(
            slot, slot, wf_send.at[direction, n], wf_recv.at[direction, n], seq=target
        )

    def spread_weight():
        load_w.wait()
        for n in range(W_PIECES):
            wx_copy(x, n, 0, right).start()
            wx_copy(x, (n + W_PIECES // 2) % W_PIECES, 1, left).start()

    def relay_weight(n):
        wx_copy((x + 3) % NX, n, 0, right).wait_recv()
        wf_copy((x + 3) % NX, n, 0, right).start()
        wx_copy((x + 1) % NX, n + W_PIECES // 2, 1, left).wait_recv()
        wf_copy((x + 1) % NX, n, 1, left).start()

    def finish_near():
        for n in range(W_PIECES // 2):
            wx_copy((x + 3) % NX, n + W_PIECES // 2, 0, right).wait_recv()
            wx_copy((x + 1) % NX, n, 1, left).wait_recv()

    def finish_far():
        for n in range(W_PIECES // 2):
            wf_copy(opposite, n, 0, right).wait_recv()
            wf_copy(opposite, n, 1, left).wait_recv()

    own = span_ref[pool_at, me]
    begin = jnp.int32(0)
    first = jnp.int32(0)
    dec_first, dec_count, dec_tail, dec_no, holds = (jnp.int32(0),) * 5
    for r in range(requests):
        count = counts_ref[pool_at, r]
        first = jnp.where(begin <= own, begin, first)
        match = dest_ref[pool_at, r] == me
        dec_first = jnp.where(match, begin, dec_first)
        dec_count = jnp.where(match, count, dec_count)
        dec_tail = jnp.where(match, tails_ref[pool_at, r], dec_tail)
        dec_no = jnp.where(match, r, dec_no)
        holds = jnp.where(match, 1, holds)
        begin = begin + count

    width = 2 * HD

    def attend(zb, diagonal):
        keys = kv[pl.ds(zb * NX, NX), 0].reshape(NX * span, HD)
        values = kv[pl.ds(zb * NX, NX), 1].reshape(NX * span, HD)
        turned = jnp.transpose(values)
        pages = [span_ref[pool_at, zb * NX + j] for j in range(NX)]
        if diagonal:
            ahead = lax.broadcasted_iota(jnp.int32, (span, width), 0) - (
                lax.broadcasted_iota(jnp.int32, (span, width), 1) % span
            )
        for pair in range(REPEAT // 2):
            scores = matmul_nt(keys, rows_of[pair])
            blocks = [scores[j * span : (j + 1) * span] for j in range(NX)]
            if diagonal:
                blocks = [
                    jnp.where(
                        ahead <= jnp.where(page >= first, (own - page) * span, -2 * span),
                        block,
                        NEG_FILL,
                    )
                    for page, block in zip(pages, blocks)
                ]
                peaks = [jnp.max(block, axis=0, keepdims=True) for block in blocks]
            else:
                seen = [(page >= first) & (page < own) for page in pages]
                peaks = [
                    jnp.where(is_seen, jnp.max(block, axis=0, keepdims=True), NEG_FILL)
                    for is_seen, block in zip(seen, blocks)
                ]
            new_high = jnp.maximum(
                jnp.maximum(peaks[0], peaks[1]), jnp.maximum(peaks[2], peaks[3])
            )
            if not diagonal:
                old_high = high_of[pair, 0:1]
                new_high = jnp.maximum(new_high, old_high)
            weights = []
            sums = []
            for j, block in enumerate(blocks):
                base = new_high if diagonal else jnp.where(seen[j], new_high, FAR_FILL)
                weights.append(jnp.exp2((block - base) * FACTOR))
                sums.append(jnp.sum(weights[-1], axis=0, keepdims=True))
            total = (sums[0] + sums[1]) + (sums[2] + sums[3])
            update = jnp.dot(
                turned, jnp.concatenate(weights, axis=0).astype(BF16), preferred_element_type=F32
            )
            if not diagonal:
                fade = jnp.exp2((old_high - new_high) * FACTOR)
                total = total + total_of[pair, 0:1] * fade
                update = update + accum[pair] * fade
            high_of[pair, 0:1] = new_high
            total_of[pair, 0:1] = total
            accum[pair] = update

    lag = 1 + jnp.where((z > 1) & (z < nz - 2), 1, 0)

    load_q.wait()
    for pair in range(REPEAT // 2):
        for n in range(2):
            h = 2 * pair + n
            rows_of[pair, n * span : (n + 1) * span, :] = q_in[:, h * HD : (h + 1) * HD]

    def far_wait(zb):
        kf_copy(zb, opposite, 0, right).wait_recv()
        kf_copy(zb, opposite, 1, left).wait_recv()

    def gather_step(t, carry):
        low, high = z - t, z + t

        for zb, direction in ((low, 0), (high, 1)):

            @pl.when((zb >= 0) & (zb < nz))
            def _():
                @pl.when(t > 0)
                def _():
                    for which in range(2):
                        kz_copy(zb, which, direction, 1).wait_recv()

                kz_sends(zb, direction, lambda copy: copy.start())

        @pl.when(low >= 0)
        def _():
            spread(low)

        @pl.when((t > 0) & (high < nz))
        def _():
            spread(high)

        past = t - lag

        @pl.when((past >= 0) & (z - past >= 0))
        def _():
            relay(z - past)

        @pl.when((past > 0) & (z + past < nz))
        def _():
            relay(z + past)

        @pl.when(t == W_START)
        def _():
            spread_weight()

        ready = t - lag - 2

        @pl.when(ready == 0)
        def _():
            far_wait(z)
            attend(z, True)

        for sign in (-1, 1):
            zb = z + sign * ready

            @pl.when((ready > 0) & (zb >= 0) & (zb < nz))
            def _():
                far_wait(zb)
                attend(zb, False)

        return carry

    lax.fori_loop(0, nz + 3, gather_step, 0)

    for pair in range(REPEAT // 2):
        result = accum[pair] / total_of[pair, 0:1]
        for n in range(2):
            h = 2 * pair + n
            block = jnp.transpose(result[:, n * span : (n + 1) * span]).astype(BF16)
            for s in range(2):
                heads_out[z, s, :, h * HD : (h + 1) * HD] = block[s * part : (s + 1) * part]

    def az_copy(zb, s, direction, target):
        slot = heads_out.at[zb, s]
        return remote(slot, slot, az_send.at[direction, zb, s], az_recv.at[zb, s], seq=target)

    def z_step(t, carry):
        low, high = z - t, z + t
        for s in range(2):

            @pl.when((t > 0) & (low >= 0))
            def _():
                az_copy(low, s, 0, me).wait_recv()

            @pl.when((low >= 0) & (z < nz - 1))
            def _():
                az_copy(low, s, 0, me + NX).start()

            @pl.when((t > 0) & (high < nz))
            def _():
                az_copy(high, s, 1, me).wait_recv()

            @pl.when((high < nz) & (z > 0))
            def _():
                az_copy(high, s, 1, me - NX).start()

        return carry

    z_step(0, 0)

    for load in load_dec:
        load.wait()
    queries = dq_ref[pool_at, dec_no].astype(F32)
    for h in range(REPEAT):
        dec_rows[h * steps : (h + 1) * steps, :] = queries[:, h * HD : (h + 1) * HD]
    rows = dec_rows[...].astype(BF16)
    new_page[...] = jnp.zeros_like(new_page)
    new_page[0, :steps, :] = dk_ref[pool_at, dec_no].astype(F32)
    new_page[1, :steps, :] = dv_ref[pool_at, dec_no].astype(F32)
    row_count = rows.shape[0]
    lane = lax.broadcasted_iota(jnp.int32, (row_count, span), 1)
    step_of = lax.broadcasted_iota(jnp.int32, (row_count, span), 0) % steps
    new_scores = jnp.where(
        lane <= step_of, matmul_nt(rows, new_page[0].astype(BF16)), NEG_FILL
    )
    live = (dec_count - 1) * span + dec_tail
    old_scores = []
    for zb in range(nz):
        keys = kv[zb * NX : (zb + 1) * NX, 0].reshape(NX * span, HD)
        scores = matmul_nt(rows, keys)
        for j in range(NX):
            page = span_ref[pool_at, zb * NX + j] - dec_first
            limit = jnp.where((page >= 0) & (page < dec_count), live - page * span, 0)
            old_scores.append(
                jnp.where(lane < limit, scores[:, j * span : (j + 1) * span], NEG_FILL)
            )
    peak = new_scores
    for block in old_scores:
        peak = jnp.maximum(peak, block)
    peak = jnp.max(peak, axis=1, keepdims=True)
    new_weights = jnp.exp2((new_scores - peak) * FACTOR)
    weight_sum = new_weights
    answer = jnp.dot(
        new_weights.astype(BF16), new_page[1].astype(BF16), preferred_element_type=F32
    )
    for zb in range(nz):
        row_weights = [
            jnp.exp2((old_scores[zb * NX + j] - peak) * FACTOR) for j in range(NX)
        ]
        for block in row_weights:
            weight_sum = weight_sum + block
        answer = answer + jnp.dot(
            jnp.concatenate(row_weights, axis=1).astype(BF16),
            kv[zb * NX : (zb + 1) * NX, 1].reshape(NX * span, HD),
            preferred_element_type=F32,
        )
    answer = answer / jnp.sum(weight_sum, axis=1, keepdims=True)
    dec_rows[...] = jnp.where(holds == 1, answer, 0.0)
    dec_out[...] = jnp.zeros_like(dec_out)
    for h in range(REPEAT):
        dec_out[:steps, h * HD : (h + 1) * HD] = dec_rows[
            h * steps : (h + 1) * steps, :
        ].astype(BF16)
    pool_copy = remote(dec_out, dec_in, pool_send.at[0], pool_recv.at[0], pool=1 - pool_at)
    pool_copy.start()
    relay_weight(0)

    edge = jnp.minimum(z, nz - 1 - z)

    def bits(value, shift, mask):
        return lax.shift_right_logical(value, shift) & mask

    def unit_code(index):
        words = [
            sum(code << 8 * n for n, code in enumerate(UNITS[i : i + 4]))
            for i in range(0, len(UNITS), 4)
        ]
        values = [jnp.int32(word) for word in words]
        level = 2
        while len(values) > 1:
            odd = bits(index, level, 1) == 1
            values = [
                jnp.where(odd, values[n + 1], values[n]) for n in range(0, len(values), 2)
            ]
            level += 1
        return bits(values[0], (index & 3) * 8, 255)

    def place_of(unit):
        code = unit_code(unit)
        k, turn = bits(code, 2, 7), code & 3
        near = bits(k + 1, 1, 7)
        paired = jnp.where((k & 1) == 1, z - near, z + near)
        beyond = jnp.where(z < nz // 2, z + k - edge, z - k + edge)
        zb = jnp.where(k <= 2 * edge, paired, beyond)
        quarter = (x + turn + jnp.where(turn == 1, 2, jnp.where(turn == 0, 0, 3))) & 3
        owner = bits(zb, 1, 7)
        toward = 1 - 2 * (quarter & 1)
        rank = ((y - owner) * toward + 4) & 3
        return (zb & 1) == core, zb, quarter, owner, toward, rank, owner * NX + quarter

    def core_copy(slot):
        return remote(
            core_out.at[slot], core_in.at[slot], core_send.at[slot], core_recv.at[slot], tp=sibling
        )

    def project(unit):
        mine, zb, quarter, _, _, _, slot = place_of(unit)
        block = heads_out[zb].reshape(span, heads_out.shape[3])
        product = jnp.dot(block, weight[quarter], preferred_element_type=F32)

        @pl.when(mine)
        def _():
            stash[slot] = product

        @pl.when(jnp.logical_not(mine))
        def _():
            core_out[slot] = product.astype(BF16)
            core_copy(slot).start()

    def y_copy(slot, dst, recv_sem, target):
        return remote(y_out.at[slot], dst, y_send.at[slot], recv_sem, tp=target * 2 + core)

    def pair_sum(unit, carry):
        mine, _, quarter, owner, toward, rank, slot = place_of(unit)

        @pl.when(mine)
        def _():
            core_copy(slot).wait_recv()
            value = stash[slot] + core_in[slot].astype(F32)

            @pl.when(rank < 2)
            def _():
                stash[slot] = value

            @pl.when(rank >= 2)
            def _():
                y_out[slot] = value.astype(BF16)

            @pl.when(rank == 2)
            def _():
                y_copy(
                    slot, relay_in.at[quarter], relay_recv.at[quarter], (owner + toward + 4) & 3
                ).start()

            @pl.when(rank == 3)
            def _():
                y_copy(
                    slot, owner_in.at[quarter, 1], owner_recv.at[quarter, 1], owner
                ).start()

        return carry

    def relay_sum(unit, carry):
        mine, _, quarter, owner, _, rank, slot = place_of(unit)

        @pl.when(mine & (rank == 1))
        def _():
            y_copy(slot, relay_in.at[quarter], relay_recv.at[quarter], y).wait_recv()
            y_out[slot] = (stash[slot] + relay_in[quarter].astype(F32)).astype(BF16)
            y_copy(slot, owner_in.at[quarter, 0], owner_recv.at[quarter, 0], owner).start()

        return carry

    def x_copy(quarter, source, target):
        distance = (target + NX - source) & 3
        return remote(
            x_out.at[quarter],
            x_in.at[source],
            x_send.at[distance],
            x_recv.at[distance],
            seq=z * NX + target,
        )

    def finish(source, value):
        row = pl.ds(source * span, span)
        out_ref[row, :] = (value.astype(F32) + resid[row, :].astype(F32)).astype(BF16)

    def owner_sum(unit, carry):
        mine, _, quarter, _, _, rank, slot = place_of(unit)

        @pl.when(mine & (rank == 0))
        def _():
            for n in range(2):
                y_copy(slot, owner_in.at[quarter, n], owner_recv.at[quarter, n], y).wait_recv()
            total = (
                stash[slot]
                + owner_in[quarter, 0].astype(F32)
                + owner_in[quarter, 1].astype(F32)
            )

            @pl.when(quarter == x)
            def _():
                finish(x, total)

            @pl.when(quarter != x)
            def _():
                x_out[quarter] = total.astype(BF16)
                x_copy(quarter, x, quarter).start()

        return carry

    count = len(UNITS)

    def clipped(value):
        return jnp.clip(value, 0, count)

    def pairs_by(unit):
        done = jnp.where(unit >= count, unit, unit - PAIR_LAG)
        for at in STEP_AT[7:]:
            done = jnp.where((edge == 0) & (unit >= at), jnp.maximum(done, at), done)
        return clipped(done)

    last = STEP_AT[-1]

    def relays_by(unit):
        return clipped(jnp.where(unit >= last, unit - 4, unit - RELAY_LAG))

    def owners_by(unit):
        done = jnp.where((unit >= last) & (edge > 0), unit - 8, unit - OWNER_LAG)
        return clipped(jnp.where(unit > count, unit - 4, done))

    def steps_by(unit):
        done = jnp.int32(0)
        for t in range(1, nz):
            at = jnp.int32(STEP_AT[t])
            if t == 5:
                at = at - jnp.where((edge == 1) | (edge == 2), 2, 0)
            done = done + jnp.where(unit >= at, 1, 0)
        return done

    def advance(t, carry):
        z_step(t, 0)

        @pl.when(t == 1)
        def _():
            relay_weight(1)

        return carry

    def unit_step(unit, carry):
        pairs, relays, owners, z_steps = carry
        new_pairs, new_relays = pairs_by(unit), relays_by(unit)
        new_owners, new_steps = owners_by(unit), steps_by(unit)
        lax.fori_loop(pairs, new_pairs, pair_sum, 0)
        lax.fori_loop(relays, new_relays, relay_sum, 0)
        lax.fori_loop(owners, new_owners, owner_sum, 0)
        lax.fori_loop(z_steps + 1, new_steps + 1, advance, 0)

        @pl.when(unit == NEAR_AT)
        def _():
            finish_near()

        @pl.when(unit == FAR_AT)
        def _():
            finish_far()

        @pl.when(unit < count)
        def _():
            project(unit)

        return (new_pairs, new_relays, new_owners, new_steps)

    load_r.wait()
    lax.fori_loop(0, count + 6, unit_step, (jnp.int32(0),) * 4)

    for distance in range(1, NX):
        source = (x + NX - distance) % NX
        x_copy(x, source, x).wait_recv()
        finish(source, x_in[source])

    pool_copy.wait()
    dec_ref[...] = dec_in[:steps, :]

    def drain(zb, carry):
        for direction in range(2):
            kz_sends(zb, direction, lambda copy: copy.wait_send())

        @pl.when((zb <= z) & (z < nz - 1))
        def _():
            for s in range(2):
                az_copy(zb, s, 0, me).wait_send()

        @pl.when((zb >= z) & (z > 0))
        def _():
            for s in range(2):
                az_copy(zb, s, 1, me).wait_send()

        kx_copy(zb, x, 0, right).wait_send()
        kx_copy(zb, x, 1, left).wait_send()
        kf_copy(zb, opposite, 0, right).wait_send()
        kf_copy(zb, opposite, 1, left).wait_send()

        for quarter in range(NX):
            slot = (zb // 2) * NX + quarter

            @pl.when(zb % 2 != core)
            def _():
                core_copy(slot).wait_send()

            @pl.when((zb % 2 == core) & (zb // 2 != y))
            def _():
                y_copy(slot, relay_in.at[quarter], relay_recv.at[quarter], y).wait_send()

        return carry

    lax.fori_loop(0, nz, drain, 0)
    for n in range(W_PIECES):
        wx_copy(x, n, 0, right).wait_send()
        wx_copy(x, n, 1, left).wait_send()
    for n in range(W_PIECES // 2):
        wf_copy(opposite, n, 0, right).wait_send()
        wf_copy(opposite, n, 1, left).wait_send()
    for distance in range(1, NX):
        target = (x + distance) % NX
        x_copy(target, x, target).wait_send()


def per_device(
    q_pre,
    k_pre,
    v_pre,
    out_weight,
    residual,
    span_ids,
    page_counts,
    tail_rows,
    dest_group,
    dec_q,
    dec_k,
    dec_v,
):
    count = lax.axis_size("seq")
    nz = count // NX
    span, features = q_pre.shape[1:]
    depth, columns = out_weight.shape
    steps = dec_q.shape[2]
    part = span // 2
    slots = nz // 2 * NX
    pairs = REPEAT // 2
    dma = pltpu.SemaphoreType.DMA
    vmem, smem, hbm = (
        pl.BlockSpec(memory_space=space) for space in (pltpu.VMEM, pltpu.SMEM, pltpu.HBM)
    )
    tile = (span, columns)
    mixed, decoded = pl.pallas_call(
        kernel,
        out_shape=(
            jax.ShapeDtypeStruct(residual.shape[1:], BF16),
            jax.ShapeDtypeStruct((steps, features), BF16),
        ),
        in_specs=[smem] * 4 + [hbm] * 8,
        out_specs=(vmem, vmem),
        scratch_shapes=[
            pltpu.VMEM(dec_q.shape, BF16),
            pltpu.VMEM(dec_k.shape, BF16),
            pltpu.VMEM(dec_v.shape, BF16),
            pltpu.VMEM((count, 2, span, HD), BF16),
            pltpu.VMEM((span, features), BF16),
            pltpu.VMEM((pairs, 2 * span, HD), BF16),
            pltpu.VMEM((pairs, 8, 2 * span), F32),
            pltpu.VMEM((pairs, 8, 2 * span), F32),
            pltpu.VMEM((pairs, HD, 2 * span), F32),
            pltpu.VMEM((nz, 2, part, features), BF16),
            pltpu.VMEM((NX, depth, columns), BF16),
            pltpu.VMEM(residual.shape[1:], BF16),
            pltpu.VMEM((slots,) + tile, BF16),
            pltpu.VMEM((slots,) + tile, BF16),
            pltpu.VMEM((slots,) + tile, F32),
            pltpu.VMEM((slots,) + tile, BF16),
            pltpu.VMEM((NX,) + tile, BF16),
            pltpu.VMEM((NX, 2) + tile, BF16),
            pltpu.VMEM((NX,) + tile, BF16),
            pltpu.VMEM((NX,) + tile, BF16),
            pltpu.VMEM((steps * REPEAT, HD), F32),
            pltpu.VMEM((2, span, HD), F32),
            pltpu.VMEM((16, features), BF16),
            pltpu.VMEM((16, features), BF16),
            dma((8,)),
            dma((2, nz, 4)),
            dma((nz, 2)),
            dma((2, nz)),
            dma((2, nz)),
            dma((2, nz)),
            dma((2, nz)),
            dma((2, W_PIECES)),
            dma((2, W_PIECES)),
            dma((2, W_PIECES // 2)),
            dma((2, W_PIECES // 2)),
            dma((2, nz, 2)),
            dma((nz, 2)),
            dma((slots,)),
            dma((slots,)),
            dma((slots,)),
            dma((NX,)),
            dma((NX, 2)),
            dma((NX,)),
            dma((NX,)),
            dma((1,)),
            dma((1,)),
        ],
        compiler_params=pltpu.CompilerParams(
            collective_id=0, has_side_effects=True, vmem_limit_bytes=60 << 20
        ),
    )(
        span_ids,
        page_counts,
        tail_rows,
        dest_group,
        dec_q,
        dec_k,
        dec_v,
        k_pre[0],
        v_pre[0],
        q_pre[0],
        out_weight,
        residual[0],
    )
    return (mixed[None], decoded[None, None])


def solution(mesh):
    placed = (
        P("pool", "seq", "tp"),
        P("pool", "seq", "tp"),
        P("pool", "seq", "tp"),
        P("tp", "seq"),
        P("pool", "tp", "seq"),
        P(),
        P(),
        P(),
        P(),
        P(None, None, None, "tp"),
        P(None, None, None, "tp"),
        P(None, None, None, "tp"),
    )
    return jax.shard_map(
        per_device,
        mesh=mesh,
        in_specs=placed,
        out_specs=(P("pool", "tp", "seq"), P("pool", "seq", None, "tp")),
        check_vma=False,
    )
```

```python
import math

import jax
import jax.numpy as jnp
from jax import lax
from jax.experimental import pallas as pl
from jax.experimental.pallas import tpu as pltpu
from jax.sharding import PartitionSpec as P

HD = 128
QH = 64
KVH = 8
REPEAT = QH // KVH
NX = 4
NEG_FILL = -1e30
FAR_FILL = 1e30
FACTOR = math.log2(math.e) / math.sqrt(HD)
MESH = pl.DeviceIdType.MESH
F32 = jnp.float32
BF16 = jnp.bfloat16
W_PIECES = 4
W_START = 8
PAIR_LAG = 2
RELAY_LAG = 8
OWNER_LAG = 12


def unit(block, *turns):
    return [block * 4 + turn for turn in turns]


SEGMENTS = [
    unit(0, 0),
    unit(1, 0),
    unit(2, 0) + unit(0, 1, 2) + unit(1, 1, 2),
    unit(3, 0) + unit(2, 1, 2) + unit(3, 1, 2),
    unit(0, 3) + unit(4, 0, 1) + unit(1, 3) + unit(4, 2) + unit(2, 3) + unit(3, 3) + unit(4, 3),
    unit(5, 3, 1, 2, 0),
    unit(6, 3, 1, 2, 0),
    unit(7, 3, 1, 2, 0),
]
UNITS = sum(SEGMENTS, [])
STEP_AT = [sum(len(segment) for segment in SEGMENTS[:t]) for t in range(len(SEGMENTS))]
NEAR_AT = UNITS.index(1)
FAR_AT = UNITS.index(3)


def matmul_nt(a, b):
    return lax.dot_general(a, b, (((1,), (1,)), ((), ())), preferred_element_type=F32)


def remote(src, dst, send_sem, recv_sem, **target):
    return pltpu.make_async_remote_copy(
        src_ref=src,
        dst_ref=dst,
        send_sem=send_sem,
        recv_sem=recv_sem,
        device_id=target,
        device_id_type=MESH,
    )


def kernel(
    span_ref,
    counts_ref,
    tails_ref,
    dest_ref,
    dq_hbm,
    dk_hbm,
    dv_hbm,
    k_hbm,
    v_hbm,
    q_hbm,
    w_hbm,
    res_hbm,
    out_ref,
    dec_ref,
    dq_ref,
    dk_ref,
    dv_ref,
    kv,
    q_in,
    rows_of,
    high_of,
    total_of,
    accum,
    heads_out,
    weight,
    resid,
    core_out,
    core_in,
    stash,
    y_out,
    relay_in,
    owner_in,
    x_out,
    x_in,
    dec_rows,
    new_page,
    dec_out,
    dec_in,
    local_sem,
    kz_send,
    kz_recv,
    kx_send,
    kx_recv,
    kf_send,
    kf_recv,
    wx_send,
    wx_recv,
    wf_send,
    wf_recv,
    az_send,
    az_recv,
    core_send,
    core_recv,
    y_send,
    relay_recv,
    owner_recv,
    x_send,
    x_recv,
    pool_send,
    pool_recv,
):
    me = lax.axis_index("seq")
    tp_at = lax.axis_index("tp")
    pool_at = lax.axis_index("pool")
    nz = kv.shape[0] // NX
    ny = NX
    span = kv.shape[2]
    z, x = me // NX, me % NX
    y, core = tp_at // 2, tp_at % 2
    right, left = z * NX + (x + 1) % NX, z * NX + (x + 3) % NX
    opposite = (x + 2) % NX
    sibling = tp_at + 1 - 2 * core
    part = heads_out.shape[2]
    steps = dec_ref.shape[0]
    requests = counts_ref.shape[1]

    load_k = pltpu.make_async_copy(k_hbm, kv.at[me, 0], local_sem.at[0])
    load_v = pltpu.make_async_copy(v_hbm, kv.at[me, 1], local_sem.at[1])
    load_q = pltpu.make_async_copy(q_hbm, q_in, local_sem.at[2])
    load_w = pltpu.make_async_copy(w_hbm, weight.at[x], local_sem.at[3])
    load_r = pltpu.make_async_copy(res_hbm, resid, local_sem.at[4])
    load_dec = [
        pltpu.make_async_copy(src, dst, local_sem.at[5 + n])
        for n, (src, dst) in enumerate(((dq_hbm, dq_ref), (dk_hbm, dk_ref), (dv_hbm, dv_ref)))
    ]
    for load in (load_k, load_v, load_q, load_w, load_r, *load_dec):
        load.start()

    barrier = pltpu.get_barrier_semaphore()

    def greet(**target):
        pl.semaphore_signal(barrier, inc=1, device_id=target, device_id_type=MESH)

    for distance in range(1, NX):
        greet(seq=z * NX + (x + distance) % NX)
        greet(tp=((y + distance) % ny) * 2 + core)
    greet(tp=sibling)
    greet(pool=1 - pool_at)

    around = 0
    for distance in (1, 2):
        for sign in (-1, 1):
            there = (z + sign * distance >= 0) & (z + sign * distance < nz)
            around = around + jnp.where(there, 1, 0)

            @pl.when(there)
            def _():
                greet(seq=me + sign * distance * NX)

    load_k.wait()
    load_v.wait()
    pl.semaphore_wait(barrier, 8 + around)

    def kz_copy(zb, which, direction, distance):
        slot = kv.at[zb * NX + x, which]
        return remote(
            slot,
            slot,
            kz_send.at[direction, zb, which * 2 + distance - 1],
            kz_recv.at[zb, which],
            seq=me + (1 - 2 * direction) * distance * NX,
        )

    def kz_sends(zb, direction, act):
        travelled = (z - zb) * (1 - 2 * direction)
        for which in range(2):
            for distance in (1, 2):
                target = z + (1 - 2 * direction) * distance

                @pl.when(
                    (travelled >= 0) & ((travelled & 1) == 0) & (target >= 0) & (target < nz)
                )
                def _():
                    act(kz_copy(zb, which, direction, distance))

    def kx_copy(zb, xb, direction, target):
        slot = kv.at[zb * NX + xb]
        return remote(
            slot, slot, kx_send.at[direction, zb], kx_recv.at[direction, zb], seq=target
        )

    def kf_copy(zb, xb, direction, target):
        slot = kv.at[zb * NX + xb, direction]
        return remote(
            slot, slot, kf_send.at[direction, zb], kf_recv.at[direction, zb], seq=target
        )

    def spread(zb):
        kx_copy(zb, x, 0, right).start()
        kx_copy(zb, x, 1, left).start()

    def relay(zb):
        kx_copy(zb, (x + 3) % NX, 0, right).wait_recv()
        kf_copy(zb, (x + 3) % NX, 0, right).start()
        kx_copy(zb, (x + 1) % NX, 1, left).wait_recv()
        kf_copy(zb, (x + 1) % NX, 1, left).start()

    height = weight.shape[1] // W_PIECES

    def w_piece(xb, piece):
        return weight.at[xb, pl.ds(piece * height, height)]

    def wx_copy(xb, piece, direction, target):
        slot = w_piece(xb, piece)
        return remote(
            slot, slot, wx_send.at[direction, piece], wx_recv.at[direction, piece], seq=target
        )

    def wf_copy(xb, n, direction, target):
        slot = w_piece(xb, direction * (W_PIECES // 2) + n)
        return remote(
            slot, slot, wf_send.at[direction, n], wf_recv.at[direction, n], seq=target
        )

    def spread_weight():
        load_w.wait()
        for n in range(W_PIECES):
            wx_copy(x, n, 0, right).start()
            wx_copy(x, (n + W_PIECES // 2) % W_PIECES, 1, left).start()

    def relay_weight(n):
        wx_copy((x + 3) % NX, n, 0, right).wait_recv()
        wf_copy((x + 3) % NX, n, 0, right).start()
        wx_copy((x + 1) % NX, n + W_PIECES // 2, 1, left).wait_recv()
        wf_copy((x + 1) % NX, n, 1, left).start()

    def finish_near():
        for n in range(W_PIECES // 2):
            wx_copy((x + 3) % NX, n + W_PIECES // 2, 0, right).wait_recv()
            wx_copy((x + 1) % NX, n, 1, left).wait_recv()

    def finish_far():
        for n in range(W_PIECES // 2):
            wf_copy(opposite, n, 0, right).wait_recv()
            wf_copy(opposite, n, 1, left).wait_recv()

    own = span_ref[pool_at, me]
    begin = jnp.int32(0)
    first = jnp.int32(0)
    dec_first, dec_count, dec_tail, dec_no, holds = (jnp.int32(0),) * 5
    for r in range(requests):
        count = counts_ref[pool_at, r]
        first = jnp.where(begin <= own, begin, first)
        match = dest_ref[pool_at, r] == me
        dec_first = jnp.where(match, begin, dec_first)
        dec_count = jnp.where(match, count, dec_count)
        dec_tail = jnp.where(match, tails_ref[pool_at, r], dec_tail)
        dec_no = jnp.where(match, r, dec_no)
        holds = jnp.where(match, 1, holds)
        begin = begin + count

    width = 2 * HD

    def attend(zb, diagonal):
        keys = kv[pl.ds(zb * NX, NX), 0].reshape(NX * span, HD)
        values = kv[pl.ds(zb * NX, NX), 1].reshape(NX * span, HD)
        turned = jnp.transpose(values)
        pages = [span_ref[pool_at, zb * NX + j] for j in range(NX)]
        if diagonal:
            ahead = lax.broadcasted_iota(jnp.int32, (span, width), 0) - (
                lax.broadcasted_iota(jnp.int32, (span, width), 1) % span
            )
        for pair in range(REPEAT // 2):
            scores = matmul_nt(keys, rows_of[pair])
            blocks = [scores[j * span : (j + 1) * span] for j in range(NX)]
            if diagonal:
                blocks = [
                    jnp.where(
                        ahead <= jnp.where(page >= first, (own - page) * span, -2 * span),
                        block,
                        NEG_FILL,
                    )
                    for page, block in zip(pages, blocks)
                ]
                peaks = [jnp.max(block, axis=0, keepdims=True) for block in blocks]
            else:
                seen = [(page >= first) & (page < own) for page in pages]
                peaks = [
                    jnp.where(is_seen, jnp.max(block, axis=0, keepdims=True), NEG_FILL)
                    for is_seen, block in zip(seen, blocks)
                ]
            new_high = jnp.maximum(
                jnp.maximum(peaks[0], peaks[1]), jnp.maximum(peaks[2], peaks[3])
            )
            if not diagonal:
                old_high = high_of[pair, 0:1]
                new_high = jnp.maximum(new_high, old_high)
            weights = []
            sums = []
            for j, block in enumerate(blocks):
                base = new_high if diagonal else jnp.where(seen[j], new_high, FAR_FILL)
                weights.append(jnp.exp2((block - base) * FACTOR))
                sums.append(jnp.sum(weights[-1], axis=0, keepdims=True))
            total = (sums[0] + sums[1]) + (sums[2] + sums[3])
            update = jnp.dot(
                turned, jnp.concatenate(weights, axis=0).astype(BF16), preferred_element_type=F32
            )
            if not diagonal:
                fade = jnp.exp2((old_high - new_high) * FACTOR)
                total = total + total_of[pair, 0:1] * fade
                update = update + accum[pair] * fade
            high_of[pair, 0:1] = new_high
            total_of[pair, 0:1] = total
            accum[pair] = update

    lag = 1 + jnp.where((z > 1) & (z < nz - 2), 1, 0)

    load_q.wait()
    for pair in range(REPEAT // 2):
        for n in range(2):
            h = 2 * pair + n
            rows_of[pair, n * span : (n + 1) * span, :] = q_in[:, h * HD : (h + 1) * HD]

    def far_wait(zb):
        kf_copy(zb, opposite, 0, right).wait_recv()
        kf_copy(zb, opposite, 1, left).wait_recv()

    def gather_step(t, carry):
        low, high = z - t, z + t

        for zb, direction in ((low, 0), (high, 1)):

            @pl.when((zb >= 0) & (zb < nz))
            def _():
                @pl.when(t > 0)
                def _():
                    for which in range(2):
                        kz_copy(zb, which, direction, 1).wait_recv()

                kz_sends(zb, direction, lambda copy: copy.start())

        @pl.when(low >= 0)
        def _():
            spread(low)

        @pl.when((t > 0) & (high < nz))
        def _():
            spread(high)

        past = t - lag

        @pl.when((past >= 0) & (z - past >= 0))
        def _():
            relay(z - past)

        @pl.when((past > 0) & (z + past < nz))
        def _():
            relay(z + past)

        @pl.when(t == W_START)
        def _():
            spread_weight()

        ready = t - lag - 2

        @pl.when(ready == 0)
        def _():
            far_wait(z)
            attend(z, True)

        for sign in (-1, 1):
            zb = z + sign * ready

            @pl.when((ready > 0) & (zb >= 0) & (zb < nz))
            def _():
                far_wait(zb)
                attend(zb, False)

        return carry

    lax.fori_loop(0, nz + 3, gather_step, 0)

    for pair in range(REPEAT // 2):
        result = accum[pair] / total_of[pair, 0:1]
        for n in range(2):
            h = 2 * pair + n
            block = jnp.transpose(result[:, n * span : (n + 1) * span]).astype(BF16)
            for s in range(2):
                heads_out[z, s, :, h * HD : (h + 1) * HD] = block[s * part : (s + 1) * part]

    def az_copy(zb, s, direction, target):
        slot = heads_out.at[zb, s]
        return remote(slot, slot, az_send.at[direction, zb, s], az_recv.at[zb, s], seq=target)

    def z_step(t, carry):
        low, high = z - t, z + t
        for s in range(2):

            @pl.when((t > 0) & (low >= 0))
            def _():
                az_copy(low, s, 0, me).wait_recv()

            @pl.when((low >= 0) & (z < nz - 1))
            def _():
                az_copy(low, s, 0, me + NX).start()

            @pl.when((t > 0) & (high < nz))
            def _():
                az_copy(high, s, 1, me).wait_recv()

            @pl.when((high < nz) & (z > 0))
            def _():
                az_copy(high, s, 1, me - NX).start()

        return carry

    z_step(0, 0)

    for load in load_dec:
        load.wait()
    queries = dq_ref[pool_at, dec_no].astype(F32)
    for h in range(REPEAT):
        dec_rows[h * steps : (h + 1) * steps, :] = queries[:, h * HD : (h + 1) * HD]
    rows = dec_rows[...].astype(BF16)
    new_page[...] = jnp.zeros_like(new_page)
    new_page[0, :steps, :] = dk_ref[pool_at, dec_no].astype(F32)
    new_page[1, :steps, :] = dv_ref[pool_at, dec_no].astype(F32)
    row_count = rows.shape[0]
    lane = lax.broadcasted_iota(jnp.int32, (row_count, span), 1)
    step_of = lax.broadcasted_iota(jnp.int32, (row_count, span), 0) % steps
    new_scores = jnp.where(
        lane <= step_of, matmul_nt(rows, new_page[0].astype(BF16)), NEG_FILL
    )
    live = (dec_count - 1) * span + dec_tail
    old_scores = []
    for zb in range(nz):
        keys = kv[zb * NX : (zb + 1) * NX, 0].reshape(NX * span, HD)
        scores = matmul_nt(rows, keys)
        for j in range(NX):
            page = span_ref[pool_at, zb * NX + j] - dec_first
            limit = jnp.where((page >= 0) & (page < dec_count), live - page * span, 0)
            old_scores.append(
                jnp.where(lane < limit, scores[:, j * span : (j + 1) * span], NEG_FILL)
            )
    peak = new_scores
    for block in old_scores:
        peak = jnp.maximum(peak, block)
    peak = jnp.max(peak, axis=1, keepdims=True)
    new_weights = jnp.exp2((new_scores - peak) * FACTOR)
    weight_sum = new_weights
    answer = jnp.dot(
        new_weights.astype(BF16), new_page[1].astype(BF16), preferred_element_type=F32
    )
    for zb in range(nz):
        row_weights = [
            jnp.exp2((old_scores[zb * NX + j] - peak) * FACTOR) for j in range(NX)
        ]
        for block in row_weights:
            weight_sum = weight_sum + block
        answer = answer + jnp.dot(
            jnp.concatenate(row_weights, axis=1).astype(BF16),
            kv[zb * NX : (zb + 1) * NX, 1].reshape(NX * span, HD),
            preferred_element_type=F32,
        )
    answer = answer / jnp.sum(weight_sum, axis=1, keepdims=True)
    dec_rows[...] = jnp.where(holds == 1, answer, 0.0)
    dec_out[...] = jnp.zeros_like(dec_out)
    for h in range(REPEAT):
        dec_out[:steps, h * HD : (h + 1) * HD] = dec_rows[
            h * steps : (h + 1) * steps, :
        ].astype(BF16)
    pool_copy = remote(dec_out, dec_in, pool_send.at[0], pool_recv.at[0], pool=1 - pool_at)
    pool_copy.start()
    relay_weight(0)

    edge = jnp.minimum(z, nz - 1 - z)

    def bits(value, shift, mask):
        return lax.shift_right_logical(value, shift) & mask

    def unit_code(index):
        words = [
            sum(code << 8 * n for n, code in enumerate(UNITS[i : i + 4]))
            for i in range(0, len(UNITS), 4)
        ]
        values = [jnp.int32(word) for word in words]
        level = 2
        while len(values) > 1:
            odd = bits(index, level, 1) == 1
            values = [
                jnp.where(odd, values[n + 1], values[n]) for n in range(0, len(values), 2)
            ]
            level += 1
        return bits(values[0], (index & 3) * 8, 255)

    def place_of(unit):
        code = unit_code(unit)
        k, turn = bits(code, 2, 7), code & 3
        near = bits(k + 1, 1, 7)
        paired = jnp.where((k & 1) == 1, z - near, z + near)
        beyond = jnp.where(z < nz // 2, z + k - edge, z - k + edge)
        zb = jnp.where(k <= 2 * edge, paired, beyond)
        quarter = (x + turn + jnp.where(turn == 1, 2, jnp.where(turn == 0, 0, 3))) & 3
        owner = bits(zb, 1, 7)
        toward = 1 - 2 * (quarter & 1)
        rank = ((y - owner) * toward + 4) & 3
        return (zb & 1) == core, zb, quarter, owner, toward, rank, owner * NX + quarter

    def core_copy(slot):
        return remote(
            core_out.at[slot], core_in.at[slot], core_send.at[slot], core_recv.at[slot], tp=sibling
        )

    def project(unit):
        mine, zb, quarter, _, _, _, slot = place_of(unit)
        block = heads_out[zb].reshape(span, heads_out.shape[3])
        product = jnp.dot(block, weight[quarter], preferred_element_type=F32)

        @pl.when(mine)
        def _():
            stash[slot] = product

        @pl.when(jnp.logical_not(mine))
        def _():
            core_out[slot] = product.astype(BF16)
            core_copy(slot).start()

    def y_copy(slot, dst, recv_sem, target):
        return remote(y_out.at[slot], dst, y_send.at[slot], recv_sem, tp=target * 2 + core)

    def pair_sum(unit, carry):
        mine, _, quarter, owner, toward, rank, slot = place_of(unit)

        @pl.when(mine)
        def _():
            core_copy(slot).wait_recv()
            value = stash[slot] + core_in[slot].astype(F32)

            @pl.when(rank < 2)
            def _():
                stash[slot] = value

            @pl.when(rank >= 2)
            def _():
                y_out[slot] = value.astype(BF16)

            @pl.when(rank == 2)
            def _():
                y_copy(
                    slot, relay_in.at[quarter], relay_recv.at[quarter], (owner + toward + 4) & 3
                ).start()

            @pl.when(rank == 3)
            def _():
                y_copy(
                    slot, owner_in.at[quarter, 1], owner_recv.at[quarter, 1], owner
                ).start()

        return carry

    def relay_sum(unit, carry):
        mine, _, quarter, owner, _, rank, slot = place_of(unit)

        @pl.when(mine & (rank == 1))
        def _():
            y_copy(slot, relay_in.at[quarter], relay_recv.at[quarter], y).wait_recv()
            y_out[slot] = (stash[slot] + relay_in[quarter].astype(F32)).astype(BF16)
            y_copy(slot, owner_in.at[quarter, 0], owner_recv.at[quarter, 0], owner).start()

        return carry

    def x_copy(quarter, source, target):
        distance = (target + NX - source) & 3
        return remote(
            x_out.at[quarter],
            x_in.at[source],
            x_send.at[distance],
            x_recv.at[distance],
            seq=z * NX + target,
        )

    def finish(source, value):
        row = pl.ds(source * span, span)
        out_ref[row, :] = (value.astype(F32) + resid[row, :].astype(F32)).astype(BF16)

    def owner_sum(unit, carry):
        mine, _, quarter, _, _, rank, slot = place_of(unit)

        @pl.when(mine & (rank == 0))
        def _():
            for n in range(2):
                y_copy(slot, owner_in.at[quarter, n], owner_recv.at[quarter, n], y).wait_recv()
            total = (
                stash[slot]
                + owner_in[quarter, 0].astype(F32)
                + owner_in[quarter, 1].astype(F32)
            )

            @pl.when(quarter == x)
            def _():
                finish(x, total)

            @pl.when(quarter != x)
            def _():
                x_out[quarter] = total.astype(BF16)
                x_copy(quarter, x, quarter).start()

        return carry

    count = len(UNITS)

    def clipped(value):
        return jnp.clip(value, 0, count)

    def pairs_by(unit):
        done = jnp.where(unit >= count, unit, unit - PAIR_LAG)
        for at in STEP_AT[7:]:
            done = jnp.where((edge == 0) & (unit >= at), jnp.maximum(done, at), done)
        return clipped(done)

    last = STEP_AT[-1]

    def relays_by(unit):
        return clipped(jnp.where(unit >= last + 2, unit - 4, unit - RELAY_LAG))

    def owners_by(unit):
        done = jnp.where((unit >= last) & (edge > 0), unit - 8, unit - OWNER_LAG)
        return clipped(jnp.where(unit > count, unit - 4, done))

    def steps_by(unit):
        done = jnp.int32(0)
        for t in range(1, nz):
            at = jnp.int32(STEP_AT[t])
            if t == 5:
                at = at - jnp.where((edge == 1) | (edge == 2), 2, 0)
            done = done + jnp.where(unit >= at, 1, 0)
        return done

    def advance(t, carry):
        z_step(t, 0)

        @pl.when(t == 1)
        def _():
            relay_weight(1)

        return carry

    def unit_step(unit, carry):
        pairs, relays, owners, z_steps = carry
        new_pairs, new_relays = pairs_by(unit), relays_by(unit)
        new_owners, new_steps = owners_by(unit), steps_by(unit)
        lax.fori_loop(pairs, new_pairs, pair_sum, 0)
        lax.fori_loop(relays, new_relays, relay_sum, 0)
        lax.fori_loop(owners, new_owners, owner_sum, 0)
        lax.fori_loop(z_steps + 1, new_steps + 1, advance, 0)

        @pl.when(unit == NEAR_AT)
        def _():
            finish_near()

        @pl.when(unit == FAR_AT)
        def _():
            finish_far()

        @pl.when(unit < count)
        def _():
            project(unit)

        return (new_pairs, new_relays, new_owners, new_steps)

    load_r.wait()
    lax.fori_loop(0, count + 6, unit_step, (jnp.int32(0),) * 4)

    for distance in range(1, NX):
        source = (x + NX - distance) % NX
        x_copy(x, source, x).wait_recv()
        finish(source, x_in[source])

    pool_copy.wait()
    dec_ref[...] = dec_in[:steps, :]

    def drain(zb, carry):
        for direction in range(2):
            kz_sends(zb, direction, lambda copy: copy.wait_send())

        @pl.when((zb <= z) & (z < nz - 1))
        def _():
            for s in range(2):
                az_copy(zb, s, 0, me).wait_send()

        @pl.when((zb >= z) & (z > 0))
        def _():
            for s in range(2):
                az_copy(zb, s, 1, me).wait_send()

        kx_copy(zb, x, 0, right).wait_send()
        kx_copy(zb, x, 1, left).wait_send()
        kf_copy(zb, opposite, 0, right).wait_send()
        kf_copy(zb, opposite, 1, left).wait_send()

        for quarter in range(NX):
            slot = (zb // 2) * NX + quarter

            @pl.when(zb % 2 != core)
            def _():
                core_copy(slot).wait_send()

            @pl.when((zb % 2 == core) & (zb // 2 != y))
            def _():
                y_copy(slot, relay_in.at[quarter], relay_recv.at[quarter], y).wait_send()

        return carry

    lax.fori_loop(0, nz, drain, 0)
    for n in range(W_PIECES):
        wx_copy(x, n, 0, right).wait_send()
        wx_copy(x, n, 1, left).wait_send()
    for n in range(W_PIECES // 2):
        wf_copy(opposite, n, 0, right).wait_send()
        wf_copy(opposite, n, 1, left).wait_send()
    for distance in range(1, NX):
        target = (x + distance) % NX
        x_copy(target, x, target).wait_send()


def per_device(
    q_pre,
    k_pre,
    v_pre,
    out_weight,
    residual,
    span_ids,
    page_counts,
    tail_rows,
    dest_group,
    dec_q,
    dec_k,
    dec_v,
):
    count = lax.axis_size("seq")
    nz = count // NX
    span, features = q_pre.shape[1:]
    depth, columns = out_weight.shape
    steps = dec_q.shape[2]
    part = span // 2
    slots = nz // 2 * NX
    pairs = REPEAT // 2
    dma = pltpu.SemaphoreType.DMA
    vmem, smem, hbm = (
        pl.BlockSpec(memory_space=space) for space in (pltpu.VMEM, pltpu.SMEM, pltpu.HBM)
    )
    tile = (span, columns)
    mixed, decoded = pl.pallas_call(
        kernel,
        out_shape=(
            jax.ShapeDtypeStruct(residual.shape[1:], BF16),
            jax.ShapeDtypeStruct((steps, features), BF16),
        ),
        in_specs=[smem] * 4 + [hbm] * 8,
        out_specs=(vmem, vmem),
        scratch_shapes=[
            pltpu.VMEM(dec_q.shape, BF16),
            pltpu.VMEM(dec_k.shape, BF16),
            pltpu.VMEM(dec_v.shape, BF16),
            pltpu.VMEM((count, 2, span, HD), BF16),
            pltpu.VMEM((span, features), BF16),
            pltpu.VMEM((pairs, 2 * span, HD), BF16),
            pltpu.VMEM((pairs, 8, 2 * span), F32),
            pltpu.VMEM((pairs, 8, 2 * span), F32),
            pltpu.VMEM((pairs, HD, 2 * span), F32),
            pltpu.VMEM((nz, 2, part, features), BF16),
            pltpu.VMEM((NX, depth, columns), BF16),
            pltpu.VMEM(residual.shape[1:], BF16),
            pltpu.VMEM((slots,) + tile, BF16),
            pltpu.VMEM((slots,) + tile, BF16),
            pltpu.VMEM((slots,) + tile, F32),
            pltpu.VMEM((slots,) + tile, BF16),
            pltpu.VMEM((NX,) + tile, BF16),
            pltpu.VMEM((NX, 2) + tile, BF16),
            pltpu.VMEM((NX,) + tile, BF16),
            pltpu.VMEM((NX,) + tile, BF16),
            pltpu.VMEM((steps * REPEAT, HD), F32),
            pltpu.VMEM((2, span, HD), F32),
            pltpu.VMEM((16, features), BF16),
            pltpu.VMEM((16, features), BF16),
            dma((8,)),
            dma((2, nz, 4)),
            dma((nz, 2)),
            dma((2, nz)),
            dma((2, nz)),
            dma((2, nz)),
            dma((2, nz)),
            dma((2, W_PIECES)),
            dma((2, W_PIECES)),
            dma((2, W_PIECES // 2)),
            dma((2, W_PIECES // 2)),
            dma((2, nz, 2)),
            dma((nz, 2)),
            dma((slots,)),
            dma((slots,)),
            dma((slots,)),
            dma((NX,)),
            dma((NX, 2)),
            dma((NX,)),
            dma((NX,)),
            dma((1,)),
            dma((1,)),
        ],
        compiler_params=pltpu.CompilerParams(
            collective_id=0, has_side_effects=True, vmem_limit_bytes=60 << 20
        ),
    )(
        span_ids,
        page_counts,
        tail_rows,
        dest_group,
        dec_q,
        dec_k,
        dec_v,
        k_pre[0],
        v_pre[0],
        q_pre[0],
        out_weight,
        residual[0],
    )
    return (mixed[None], decoded[None, None])


def solution(mesh):
    placed = (
        P("pool", "seq", "tp"),
        P("pool", "seq", "tp"),
        P("pool", "seq", "tp"),
        P("tp", "seq"),
        P("pool", "tp", "seq"),
        P(),
        P(),
        P(),
        P(),
        P(None, None, None, "tp"),
        P(None, None, None, "tp"),
        P(None, None, None, "tp"),
    )
    return jax.shard_map(
        per_device,
        mesh=mesh,
        in_specs=placed,
        out_specs=(P("pool", "tp", "seq"), P("pool", "seq", None, "tp")),
        check_vma=False,
    )
```

```python
import math

import jax
import jax.numpy as jnp
from jax import lax
from jax.experimental import pallas as pl
from jax.experimental.pallas import tpu as pltpu
from jax.sharding import PartitionSpec as P

HD = 128
QH = 64
KVH = 8
REPEAT = QH // KVH
NX = 4
NEG_FILL = -1e30
FAR_FILL = 1e30
FACTOR = math.log2(math.e) / math.sqrt(HD)
MESH = pl.DeviceIdType.MESH
F32 = jnp.float32
BF16 = jnp.bfloat16
W_PIECES = 4
W_START = 8
PAIR_LAG = 2
RELAY_LAG = 8
OWNER_LAG = 12


def unit(block, *turns):
    return [block * 4 + turn for turn in turns]


SEGMENTS = [
    unit(0, 0),
    unit(1, 0),
    unit(2, 0) + unit(0, 1, 2) + unit(1, 1, 2),
    unit(3, 0) + unit(2, 1, 2) + unit(3, 1, 2),
    unit(0, 3) + unit(4, 0, 1) + unit(1, 3) + unit(4, 2) + unit(2, 3) + unit(3, 3) + unit(4, 3),
    unit(5, 3, 1, 2, 0),
    unit(6, 3, 1, 2, 0),
    unit(7, 3, 1, 2, 0),
]
UNITS = sum(SEGMENTS, [])
STEP_AT = [sum(len(segment) for segment in SEGMENTS[:t]) for t in range(len(SEGMENTS))]
NEAR_AT = UNITS.index(1)
FAR_AT = UNITS.index(3)


def matmul_nt(a, b):
    return lax.dot_general(a, b, (((1,), (1,)), ((), ())), preferred_element_type=F32)


def remote(src, dst, send_sem, recv_sem, **target):
    return pltpu.make_async_remote_copy(
        src_ref=src,
        dst_ref=dst,
        send_sem=send_sem,
        recv_sem=recv_sem,
        device_id=target,
        device_id_type=MESH,
    )


def kernel(
    span_ref,
    counts_ref,
    tails_ref,
    dest_ref,
    dq_hbm,
    dk_hbm,
    dv_hbm,
    k_hbm,
    v_hbm,
    q_hbm,
    w_hbm,
    res_hbm,
    out_ref,
    dec_ref,
    dq_ref,
    dk_ref,
    dv_ref,
    kv,
    q_in,
    rows_of,
    high_of,
    total_of,
    accum,
    heads_out,
    weight,
    resid,
    core_out,
    core_in,
    stash,
    y_out,
    relay_in,
    owner_in,
    x_out,
    x_in,
    dec_rows,
    new_page,
    dec_out,
    dec_in,
    local_sem,
    kz_send,
    kz_recv,
    kx_send,
    kx_recv,
    kf_send,
    kf_recv,
    wx_send,
    wx_recv,
    wf_send,
    wf_recv,
    az_send,
    az_recv,
    core_send,
    core_recv,
    y_send,
    relay_recv,
    owner_recv,
    x_send,
    x_recv,
    pool_send,
    pool_recv,
):
    me = lax.axis_index("seq")
    tp_at = lax.axis_index("tp")
    pool_at = lax.axis_index("pool")
    nz = kv.shape[0] // NX
    ny = NX
    span = kv.shape[2]
    z, x = me // NX, me % NX
    y, core = tp_at // 2, tp_at % 2
    right, left = z * NX + (x + 1) % NX, z * NX + (x + 3) % NX
    opposite = (x + 2) % NX
    sibling = tp_at + 1 - 2 * core
    part = heads_out.shape[2]
    steps = dec_ref.shape[0]
    requests = counts_ref.shape[1]

    load_k = pltpu.make_async_copy(k_hbm, kv.at[me, 0], local_sem.at[0])
    load_v = pltpu.make_async_copy(v_hbm, kv.at[me, 1], local_sem.at[1])
    load_q = pltpu.make_async_copy(q_hbm, q_in, local_sem.at[2])
    load_w = pltpu.make_async_copy(w_hbm, weight.at[x], local_sem.at[3])
    load_r = pltpu.make_async_copy(res_hbm, resid, local_sem.at[4])
    load_dec = [
        pltpu.make_async_copy(src, dst, local_sem.at[5 + n])
        for n, (src, dst) in enumerate(((dq_hbm, dq_ref), (dk_hbm, dk_ref), (dv_hbm, dv_ref)))
    ]
    for load in (load_k, load_v, load_q, load_w, load_r, *load_dec):
        load.start()

    barrier = pltpu.get_barrier_semaphore()

    def greet(**target):
        pl.semaphore_signal(barrier, inc=1, device_id=target, device_id_type=MESH)

    for distance in range(1, NX):
        greet(seq=z * NX + (x + distance) % NX)
        greet(tp=((y + distance) % ny) * 2 + core)
    greet(tp=sibling)
    greet(pool=1 - pool_at)

    around = 0
    for distance in (1, 2):
        for sign in (-1, 1):
            there = (z + sign * distance >= 0) & (z + sign * distance < nz)
            around = around + jnp.where(there, 1, 0)

            @pl.when(there)
            def _():
                greet(seq=me + sign * distance * NX)

    load_k.wait()
    load_v.wait()
    pl.semaphore_wait(barrier, 8 + around)

    def kz_copy(zb, which, direction, distance):
        slot = kv.at[zb * NX + x, which]
        return remote(
            slot,
            slot,
            kz_send.at[direction, zb, which * 2 + distance - 1],
            kz_recv.at[zb, which],
            seq=me + (1 - 2 * direction) * distance * NX,
        )

    def kz_sends(zb, direction, act):
        travelled = (z - zb) * (1 - 2 * direction)
        for which in range(2):
            for distance in (1, 2):
                target = z + (1 - 2 * direction) * distance

                @pl.when(
                    (travelled >= 0) & ((travelled & 1) == 0) & (target >= 0) & (target < nz)
                )
                def _():
                    act(kz_copy(zb, which, direction, distance))

    def kx_copy(zb, xb, direction, target):
        slot = kv.at[zb * NX + xb]
        return remote(
            slot, slot, kx_send.at[direction, zb], kx_recv.at[direction, zb], seq=target
        )

    def kf_copy(zb, xb, direction, target):
        slot = kv.at[zb * NX + xb, direction]
        return remote(
            slot, slot, kf_send.at[direction, zb], kf_recv.at[direction, zb], seq=target
        )

    def spread(zb):
        kx_copy(zb, x, 0, right).start()
        kx_copy(zb, x, 1, left).start()

    def relay(zb):
        kx_copy(zb, (x + 3) % NX, 0, right).wait_recv()
        kf_copy(zb, (x + 3) % NX, 0, right).start()
        kx_copy(zb, (x + 1) % NX, 1, left).wait_recv()
        kf_copy(zb, (x + 1) % NX, 1, left).start()

    height = weight.shape[1] // W_PIECES

    def w_piece(xb, piece):
        return weight.at[xb, pl.ds(piece * height, height)]

    def wx_copy(xb, piece, direction, target):
        slot = w_piece(xb, piece)
        return remote(
            slot, slot, wx_send.at[direction, piece], wx_recv.at[direction, piece], seq=target
        )

    def wf_copy(xb, n, direction, target):
        slot = w_piece(xb, direction * (W_PIECES // 2) + n)
        return remote(
            slot, slot, wf_send.at[direction, n], wf_recv.at[direction, n], seq=target
        )

    def spread_weight():
        load_w.wait()
        for n in range(W_PIECES):
            wx_copy(x, n, 0, right).start()
            wx_copy(x, (n + W_PIECES // 2) % W_PIECES, 1, left).start()

    def relay_weight(n):
        wx_copy((x + 3) % NX, n, 0, right).wait_recv()
        wf_copy((x + 3) % NX, n, 0, right).start()
        wx_copy((x + 1) % NX, n + W_PIECES // 2, 1, left).wait_recv()
        wf_copy((x + 1) % NX, n, 1, left).start()

    def finish_near():
        for n in range(W_PIECES // 2):
            wx_copy((x + 3) % NX, n + W_PIECES // 2, 0, right).wait_recv()
            wx_copy((x + 1) % NX, n, 1, left).wait_recv()

    def finish_far():
        for n in range(W_PIECES // 2):
            wf_copy(opposite, n, 0, right).wait_recv()
            wf_copy(opposite, n, 1, left).wait_recv()

    own = span_ref[pool_at, me]
    begin = jnp.int32(0)
    first = jnp.int32(0)
    dec_first, dec_count, dec_tail, dec_no, holds = (jnp.int32(0),) * 5
    for r in range(requests):
        count = counts_ref[pool_at, r]
        first = jnp.where(begin <= own, begin, first)
        match = dest_ref[pool_at, r] == me
        dec_first = jnp.where(match, begin, dec_first)
        dec_count = jnp.where(match, count, dec_count)
        dec_tail = jnp.where(match, tails_ref[pool_at, r], dec_tail)
        dec_no = jnp.where(match, r, dec_no)
        holds = jnp.where(match, 1, holds)
        begin = begin + count

    width = 2 * HD

    def attend(zb, diagonal):
        keys = kv[pl.ds(zb * NX, NX), 0].reshape(NX * span, HD)
        values = kv[pl.ds(zb * NX, NX), 1].reshape(NX * span, HD)
        turned = jnp.transpose(values)
        pages = [span_ref[pool_at, zb * NX + j] for j in range(NX)]
        if diagonal:
            ahead = lax.broadcasted_iota(jnp.int32, (span, width), 0) - (
                lax.broadcasted_iota(jnp.int32, (span, width), 1) % span
            )
        for pair in range(REPEAT // 2):
            scores = matmul_nt(keys, rows_of[pair])
            blocks = [scores[j * span : (j + 1) * span] for j in range(NX)]
            if diagonal:
                blocks = [
                    jnp.where(
                        ahead <= jnp.where(page >= first, (own - page) * span, -2 * span),
                        block,
                        NEG_FILL,
                    )
                    for page, block in zip(pages, blocks)
                ]
                peaks = [jnp.max(block, axis=0, keepdims=True) for block in blocks]
            else:
                seen = [(page >= first) & (page < own) for page in pages]
                peaks = [
                    jnp.where(is_seen, jnp.max(block, axis=0, keepdims=True), NEG_FILL)
                    for is_seen, block in zip(seen, blocks)
                ]
            new_high = jnp.maximum(
                jnp.maximum(peaks[0], peaks[1]), jnp.maximum(peaks[2], peaks[3])
            )
            if not diagonal:
                old_high = high_of[pair, 0:1]
                new_high = jnp.maximum(new_high, old_high)
            weights = []
            sums = []
            for j, block in enumerate(blocks):
                base = new_high if diagonal else jnp.where(seen[j], new_high, FAR_FILL)
                weights.append(jnp.exp2((block - base) * FACTOR))
                sums.append(jnp.sum(weights[-1], axis=0, keepdims=True))
            total = (sums[0] + sums[1]) + (sums[2] + sums[3])
            update = jnp.dot(
                turned, jnp.concatenate(weights, axis=0).astype(BF16), preferred_element_type=F32
            )
            if not diagonal:
                fade = jnp.exp2((old_high - new_high) * FACTOR)
                total = total + total_of[pair, 0:1] * fade
                update = update + accum[pair] * fade
            high_of[pair, 0:1] = new_high
            total_of[pair, 0:1] = total
            accum[pair] = update

    lag = 1 + jnp.where((z > 1) & (z < nz - 2), 1, 0)

    load_q.wait()
    for pair in range(REPEAT // 2):
        for n in range(2):
            h = 2 * pair + n
            rows_of[pair, n * span : (n + 1) * span, :] = q_in[:, h * HD : (h + 1) * HD]

    def far_wait(zb):
        kf_copy(zb, opposite, 0, right).wait_recv()
        kf_copy(zb, opposite, 1, left).wait_recv()

    def gather_step(t, carry):
        low, high = z - t, z + t

        for zb, direction in ((low, 0), (high, 1)):

            @pl.when((zb >= 0) & (zb < nz))
            def _():
                @pl.when(t > 0)
                def _():
                    for which in range(2):
                        kz_copy(zb, which, direction, 1).wait_recv()

                kz_sends(zb, direction, lambda copy: copy.start())

        @pl.when(low >= 0)
        def _():
            spread(low)

        @pl.when((t > 0) & (high < nz))
        def _():
            spread(high)

        past = t - lag

        @pl.when((past >= 0) & (z - past >= 0))
        def _():
            relay(z - past)

        @pl.when((past > 0) & (z + past < nz))
        def _():
            relay(z + past)

        @pl.when(t == W_START)
        def _():
            spread_weight()

        ready = t - lag - 2

        @pl.when(ready == 0)
        def _():
            far_wait(z)
            attend(z, True)

        for sign in (-1, 1):
            zb = z + sign * ready

            @pl.when((ready > 0) & (zb >= 0) & (zb < nz))
            def _():
                far_wait(zb)
                attend(zb, False)

        return carry

    lax.fori_loop(0, nz + 3, gather_step, 0)

    for pair in range(REPEAT // 2):
        result = accum[pair] / total_of[pair, 0:1]
        for n in range(2):
            h = 2 * pair + n
            block = jnp.transpose(result[:, n * span : (n + 1) * span]).astype(BF16)
            for s in range(2):
                heads_out[z, s, :, h * HD : (h + 1) * HD] = block[s * part : (s + 1) * part]

    def az_copy(zb, s, direction, target):
        slot = heads_out.at[zb, s]
        return remote(slot, slot, az_send.at[direction, zb, s], az_recv.at[zb, s], seq=target)

    def z_step(t, carry):
        low, high = z - t, z + t
        for s in range(2):

            @pl.when((t > 0) & (low >= 0))
            def _():
                az_copy(low, s, 0, me).wait_recv()

            @pl.when((low >= 0) & (z < nz - 1))
            def _():
                az_copy(low, s, 0, me + NX).start()

            @pl.when((t > 0) & (high < nz))
            def _():
                az_copy(high, s, 1, me).wait_recv()

            @pl.when((high < nz) & (z > 0))
            def _():
                az_copy(high, s, 1, me - NX).start()

        return carry

    z_step(0, 0)

    for load in load_dec:
        load.wait()
    queries = dq_ref[pool_at, dec_no].astype(F32)
    for h in range(REPEAT):
        dec_rows[h * steps : (h + 1) * steps, :] = queries[:, h * HD : (h + 1) * HD]
    rows = dec_rows[...].astype(BF16)
    new_page[...] = jnp.zeros_like(new_page)
    new_page[0, :steps, :] = dk_ref[pool_at, dec_no].astype(F32)
    new_page[1, :steps, :] = dv_ref[pool_at, dec_no].astype(F32)
    row_count = rows.shape[0]
    lane = lax.broadcasted_iota(jnp.int32, (row_count, span), 1)
    step_of = lax.broadcasted_iota(jnp.int32, (row_count, span), 0) % steps
    new_scores = jnp.where(
        lane <= step_of, matmul_nt(rows, new_page[0].astype(BF16)), NEG_FILL
    )
    live = (dec_count - 1) * span + dec_tail
    old_scores = []
    for zb in range(nz):
        keys = kv[zb * NX : (zb + 1) * NX, 0].reshape(NX * span, HD)
        scores = matmul_nt(rows, keys)
        for j in range(NX):
            page = span_ref[pool_at, zb * NX + j] - dec_first
            limit = jnp.where((page >= 0) & (page < dec_count), live - page * span, 0)
            old_scores.append(
                jnp.where(lane < limit, scores[:, j * span : (j + 1) * span], NEG_FILL)
            )
    peak = new_scores
    for block in old_scores:
        peak = jnp.maximum(peak, block)
    peak = jnp.max(peak, axis=1, keepdims=True)
    new_weights = jnp.exp2((new_scores - peak) * FACTOR)
    weight_sum = new_weights
    answer = jnp.dot(
        new_weights.astype(BF16), new_page[1].astype(BF16), preferred_element_type=F32
    )
    for zb in range(nz):
        row_weights = [
            jnp.exp2((old_scores[zb * NX + j] - peak) * FACTOR) for j in range(NX)
        ]
        for block in row_weights:
            weight_sum = weight_sum + block
        answer = answer + jnp.dot(
            jnp.concatenate(row_weights, axis=1).astype(BF16),
            kv[zb * NX : (zb + 1) * NX, 1].reshape(NX * span, HD),
            preferred_element_type=F32,
        )
    answer = answer / jnp.sum(weight_sum, axis=1, keepdims=True)
    dec_rows[...] = jnp.where(holds == 1, answer, 0.0)
    dec_out[...] = jnp.zeros_like(dec_out)
    for h in range(REPEAT):
        dec_out[:steps, h * HD : (h + 1) * HD] = dec_rows[
            h * steps : (h + 1) * steps, :
        ].astype(BF16)
    pool_copy = remote(dec_out, dec_in, pool_send.at[0], pool_recv.at[0], pool=1 - pool_at)
    pool_copy.start()
    relay_weight(0)

    edge = jnp.minimum(z, nz - 1 - z)

    def bits(value, shift, mask):
        return lax.shift_right_logical(value, shift) & mask

    def unit_code(index):
        words = [
            sum(code << 8 * n for n, code in enumerate(UNITS[i : i + 4]))
            for i in range(0, len(UNITS), 4)
        ]
        values = [jnp.int32(word) for word in words]
        level = 2
        while len(values) > 1:
            odd = bits(index, level, 1) == 1
            values = [
                jnp.where(odd, values[n + 1], values[n]) for n in range(0, len(values), 2)
            ]
            level += 1
        return bits(values[0], (index & 3) * 8, 255)

    def place_of(unit):
        code = unit_code(unit)
        k, turn = bits(code, 2, 7), code & 3
        near = bits(k + 1, 1, 7)
        paired = jnp.where((k & 1) == 1, z - near, z + near)
        beyond = jnp.where(z < nz // 2, z + k - edge, z - k + edge)
        zb = jnp.where(k <= 2 * edge, paired, beyond)
        quarter = (x + turn + jnp.where(turn == 1, 2, jnp.where(turn == 0, 0, 3))) & 3
        owner = bits(zb, 1, 7)
        toward = 1 - 2 * (quarter & 1)
        rank = ((y - owner) * toward + 4) & 3
        return (zb & 1) == core, zb, quarter, owner, toward, rank, owner * NX + quarter

    def core_copy(slot):
        return remote(
            core_out.at[slot], core_in.at[slot], core_send.at[slot], core_recv.at[slot], tp=sibling
        )

    def project(unit):
        mine, zb, quarter, _, _, _, slot = place_of(unit)
        block = heads_out[zb].reshape(span, heads_out.shape[3])
        product = jnp.dot(block, weight[quarter], preferred_element_type=F32)

        @pl.when(mine)
        def _():
            stash[slot] = product

        @pl.when(jnp.logical_not(mine))
        def _():
            core_out[slot] = product.astype(BF16)
            core_copy(slot).start()

    def y_copy(slot, dst, recv_sem, target):
        return remote(y_out.at[slot], dst, y_send.at[slot], recv_sem, tp=target * 2 + core)

    def pair_sum(unit, carry):
        mine, _, quarter, owner, toward, rank, slot = place_of(unit)

        @pl.when(mine)
        def _():
            core_copy(slot).wait_recv()
            value = stash[slot] + core_in[slot].astype(F32)

            @pl.when(rank < 2)
            def _():
                stash[slot] = value

            @pl.when(rank >= 2)
            def _():
                y_out[slot] = value.astype(BF16)

            @pl.when(rank == 2)
            def _():
                y_copy(
                    slot, relay_in.at[quarter], relay_recv.at[quarter], (owner + toward + 4) & 3
                ).start()

            @pl.when(rank == 3)
            def _():
                y_copy(
                    slot, owner_in.at[quarter, 1], owner_recv.at[quarter, 1], owner
                ).start()

        return carry

    def relay_sum(unit, carry):
        mine, _, quarter, owner, _, rank, slot = place_of(unit)

        @pl.when(mine & (rank == 1))
        def _():
            y_copy(slot, relay_in.at[quarter], relay_recv.at[quarter], y).wait_recv()
            y_out[slot] = (stash[slot] + relay_in[quarter].astype(F32)).astype(BF16)
            y_copy(slot, owner_in.at[quarter, 0], owner_recv.at[quarter, 0], owner).start()

        return carry

    def x_copy(quarter, source, target):
        distance = (target + NX - source) & 3
        return remote(
            x_out.at[quarter],
            x_in.at[source],
            x_send.at[distance],
            x_recv.at[distance],
            seq=z * NX + target,
        )

    def finish(source, value):
        row = pl.ds(source * span, span)
        out_ref[row, :] = (value.astype(F32) + resid[row, :].astype(F32)).astype(BF16)

    def owner_sum(unit, carry):
        mine, _, quarter, _, _, rank, slot = place_of(unit)

        @pl.when(mine & (rank == 0))
        def _():
            for n in range(2):
                y_copy(slot, owner_in.at[quarter, n], owner_recv.at[quarter, n], y).wait_recv()
            total = (
                stash[slot]
                + owner_in[quarter, 0].astype(F32)
                + owner_in[quarter, 1].astype(F32)
            )

            @pl.when(quarter == x)
            def _():
                finish(x, total)

            @pl.when(quarter != x)
            def _():
                x_out[quarter] = total.astype(BF16)
                x_copy(quarter, x, quarter).start()

        return carry

    count = len(UNITS)

    def clipped(value):
        return jnp.clip(value, 0, count)

    def pairs_by(unit):
        done = jnp.where(unit >= count, unit, unit - PAIR_LAG)
        for at in STEP_AT[7:]:
            done = jnp.where((edge == 0) & (unit >= at), jnp.maximum(done, at), done)
        return clipped(done)

    last = STEP_AT[-1]

    def relays_by(unit):
        return clipped(jnp.where(unit >= last + 2, unit - 4, unit - RELAY_LAG))

    def owners_by(unit):
        done = jnp.where(unit >= last + 2, unit - 8, unit - OWNER_LAG)
        return clipped(jnp.where(unit > count, unit - 4, done))

    def steps_by(unit):
        done = jnp.int32(0)
        for t in range(1, nz):
            at = jnp.int32(STEP_AT[t])
            if t == 5:
                at = at - jnp.where((edge == 1) | (edge == 2), 2, 0)
            done = done + jnp.where(unit >= at, 1, 0)
        return done

    def advance(t, carry):
        z_step(t, 0)

        @pl.when(t == 1)
        def _():
            relay_weight(1)

        return carry

    def unit_step(unit, carry):
        pairs, relays, owners, z_steps = carry
        new_pairs, new_relays = pairs_by(unit), relays_by(unit)
        new_owners, new_steps = owners_by(unit), steps_by(unit)
        lax.fori_loop(pairs, new_pairs, pair_sum, 0)
        lax.fori_loop(relays, new_relays, relay_sum, 0)
        lax.fori_loop(owners, new_owners, owner_sum, 0)
        lax.fori_loop(z_steps + 1, new_steps + 1, advance, 0)

        @pl.when(unit == NEAR_AT)
        def _():
            finish_near()

        @pl.when(unit == FAR_AT)
        def _():
            finish_far()

        @pl.when(unit < count)
        def _():
            project(unit)

        return (new_pairs, new_relays, new_owners, new_steps)

    load_r.wait()
    lax.fori_loop(0, count + 6, unit_step, (jnp.int32(0),) * 4)

    for distance in range(1, NX):
        source = (x + NX - distance) % NX
        x_copy(x, source, x).wait_recv()
        finish(source, x_in[source])

    pool_copy.wait()
    dec_ref[...] = dec_in[:steps, :]

    def drain(zb, carry):
        for direction in range(2):
            kz_sends(zb, direction, lambda copy: copy.wait_send())

        @pl.when((zb <= z) & (z < nz - 1))
        def _():
            for s in range(2):
                az_copy(zb, s, 0, me).wait_send()

        @pl.when((zb >= z) & (z > 0))
        def _():
            for s in range(2):
                az_copy(zb, s, 1, me).wait_send()

        kx_copy(zb, x, 0, right).wait_send()
        kx_copy(zb, x, 1, left).wait_send()
        kf_copy(zb, opposite, 0, right).wait_send()
        kf_copy(zb, opposite, 1, left).wait_send()

        for quarter in range(NX):
            slot = (zb // 2) * NX + quarter

            @pl.when(zb % 2 != core)
            def _():
                core_copy(slot).wait_send()

            @pl.when((zb % 2 == core) & (zb // 2 != y))
            def _():
                y_copy(slot, relay_in.at[quarter], relay_recv.at[quarter], y).wait_send()

        return carry

    lax.fori_loop(0, nz, drain, 0)
    for n in range(W_PIECES):
        wx_copy(x, n, 0, right).wait_send()
        wx_copy(x, n, 1, left).wait_send()
    for n in range(W_PIECES // 2):
        wf_copy(opposite, n, 0, right).wait_send()
        wf_copy(opposite, n, 1, left).wait_send()
    for distance in range(1, NX):
        target = (x + distance) % NX
        x_copy(target, x, target).wait_send()


def per_device(
    q_pre,
    k_pre,
    v_pre,
    out_weight,
    residual,
    span_ids,
    page_counts,
    tail_rows,
    dest_group,
    dec_q,
    dec_k,
    dec_v,
):
    count = lax.axis_size("seq")
    nz = count // NX
    span, features = q_pre.shape[1:]
    depth, columns = out_weight.shape
    steps = dec_q.shape[2]
    part = span // 2
    slots = nz // 2 * NX
    pairs = REPEAT // 2
    dma = pltpu.SemaphoreType.DMA
    vmem, smem, hbm = (
        pl.BlockSpec(memory_space=space) for space in (pltpu.VMEM, pltpu.SMEM, pltpu.HBM)
    )
    tile = (span, columns)
    mixed, decoded = pl.pallas_call(
        kernel,
        out_shape=(
            jax.ShapeDtypeStruct(residual.shape[1:], BF16),
            jax.ShapeDtypeStruct((steps, features), BF16),
        ),
        in_specs=[smem] * 4 + [hbm] * 8,
        out_specs=(vmem, vmem),
        scratch_shapes=[
            pltpu.VMEM(dec_q.shape, BF16),
            pltpu.VMEM(dec_k.shape, BF16),
            pltpu.VMEM(dec_v.shape, BF16),
            pltpu.VMEM((count, 2, span, HD), BF16),
            pltpu.VMEM((span, features), BF16),
            pltpu.VMEM((pairs, 2 * span, HD), BF16),
            pltpu.VMEM((pairs, 8, 2 * span), F32),
            pltpu.VMEM((pairs, 8, 2 * span), F32),
            pltpu.VMEM((pairs, HD, 2 * span), F32),
            pltpu.VMEM((nz, 2, part, features), BF16),
            pltpu.VMEM((NX, depth, columns), BF16),
            pltpu.VMEM(residual.shape[1:], BF16),
            pltpu.VMEM((slots,) + tile, BF16),
            pltpu.VMEM((slots,) + tile, BF16),
            pltpu.VMEM((slots,) + tile, F32),
            pltpu.VMEM((slots,) + tile, BF16),
            pltpu.VMEM((NX,) + tile, BF16),
            pltpu.VMEM((NX, 2) + tile, BF16),
            pltpu.VMEM((NX,) + tile, BF16),
            pltpu.VMEM((NX,) + tile, BF16),
            pltpu.VMEM((steps * REPEAT, HD), F32),
            pltpu.VMEM((2, span, HD), F32),
            pltpu.VMEM((16, features), BF16),
            pltpu.VMEM((16, features), BF16),
            dma((8,)),
            dma((2, nz, 4)),
            dma((nz, 2)),
            dma((2, nz)),
            dma((2, nz)),
            dma((2, nz)),
            dma((2, nz)),
            dma((2, W_PIECES)),
            dma((2, W_PIECES)),
            dma((2, W_PIECES // 2)),
            dma((2, W_PIECES // 2)),
            dma((2, nz, 2)),
            dma((nz, 2)),
            dma((slots,)),
            dma((slots,)),
            dma((slots,)),
            dma((NX,)),
            dma((NX, 2)),
            dma((NX,)),
            dma((NX,)),
            dma((1,)),
            dma((1,)),
        ],
        compiler_params=pltpu.CompilerParams(
            collective_id=0, has_side_effects=True, vmem_limit_bytes=60 << 20
        ),
    )(
        span_ids,
        page_counts,
        tail_rows,
        dest_group,
        dec_q,
        dec_k,
        dec_v,
        k_pre[0],
        v_pre[0],
        q_pre[0],
        out_weight,
        residual[0],
    )
    return (mixed[None], decoded[None, None])


def solution(mesh):
    placed = (
        P("pool", "seq", "tp"),
        P("pool", "seq", "tp"),
        P("pool", "seq", "tp"),
        P("tp", "seq"),
        P("pool", "tp", "seq"),
        P(),
        P(),
        P(),
        P(),
        P(None, None, None, "tp"),
        P(None, None, None, "tp"),
        P(None, None, None, "tp"),
    )
    return jax.shard_map(
        per_device,
        mesh=mesh,
        in_specs=placed,
        out_specs=(P("pool", "tp", "seq"), P("pool", "seq", None, "tp")),
        check_vma=False,
    )
```
